32 devices in a mesh: view: 8 (over z, y), depth: 4 (over x, core).
Axes of the slice: x: 2, y: 2, z: 4, core: 2. Of those that a mesh axis runs over, the one named last changes fastest.
Arguments:
- features: bfloat16 [24, 1024, 32], P('view'), may hold values from -6 to 6
- view_lists: int32 [24, 10], P('view'), may hold values from 0 to 15
- requests: int32 [8, 8, 2], replicated, may hold values from 0 to 2
- warp_idx: int32 [24, 10, 64, 8, 128], P('view', None, None, 'depth'), may hold values from -682 to 1023
- conv_weight: bfloat16 [27, 8, 8], replicated, may hold values from -0.4375 to 0.4375
Outputs:
- regularized: bfloat16 [24, 8, 64, 8, 128], P('view', None, 'depth')
The draws below stay inside these ranges and needn't reach their ends.
Inputs may be any that keep to these rules, and one draw needn't show every extreme that they name: `warp_idx`: A negative entry marks a sample that falls outside the source tile and is left out of the sum and the count.
All inputs are finite; a program needn't handle non-finite values.
Results may differ from the reference program's by a relative error of at most 0.0049.
Values may be sent and summed in bfloat16 or wider, within the bound.
A program may use at most 128 MiB of HBM per device.

```python
import jax
import jax.numpy as jnp
from jax import lax

CHANNELS = 32
GROUPS = 8
DEPTH = 64
SOURCES = 10
CAP = 2
TILE_H = 8
TILE_W = 128
VIEW_DEV = 3
VIEWS = 24
PIX = 1024
N_VIEW = 8


def with_ends(values, key, smallest, top_value):
    spot = [jax.random.randint(jax.random.fold_in(key, axis), (), 0, length) for axis, length in enumerate(values.shape)]
    widest = values.shape.index(max(values.shape))
    beside = spot[:widest] + [(spot[widest] + 1) % values.shape[widest]] + spot[widest + 1:]
    return values.at[tuple(spot)].set(smallest).at[tuple(beside)].set(top_value)


def levels(stream_key, dims, shards, smallest, high):
    level = 1.0
    for position, shards_of in shards:
        draws = jax.random.uniform(jax.random.fold_in(jax.random.fold_in(stream_key, 6), position), (shards_of,), jnp.float32, smallest / len(shards), high / len(shards))
        level = level * jnp.repeat(jnp.exp(draws), dims[position] // shards_of).reshape((-1,) + (1,) * (len(dims) - 1 - position))
    return level


def noise(rng, dims, width, bound, pieces=(), held_as=jnp.bfloat16):
    array = jax.random.normal(rng, dims, jnp.float32) * width
    if len(pieces) > 0:
        array = levels(rng, dims, pieces, -0.22, 0.18) * array
    return jnp.clip(array, min=-bound, max=bound).astype(held_as)


def setup_inputs(seed: int = 0) -> dict:
    key_of = jax.random.split(jax.random.key(seed), 6)
    features = noise(key_of[0], (VIEWS, PIX, CHANNELS), 1.0, 6.0, ((0, 8),))
    view_lists = with_ends(jax.random.randint(key_of[1], (VIEWS, SOURCES), 0, N_VIEW * CAP), jax.random.fold_in(key_of[1], 1), 0, (N_VIEW * CAP) - 1).astype(jnp.int32)
    requests = with_ends(jax.random.randint(key_of[2], (N_VIEW, N_VIEW, CAP), 0, VIEW_DEV), jax.random.fold_in(key_of[2], 1), 0, VIEW_DEV - 1).astype(jnp.int32)
    warp_idx = with_ends(jax.random.randint(key_of[3], (VIEWS, SOURCES, DEPTH, TILE_H, TILE_W), 0 - (2 * PIX) // 3, PIX), jax.random.fold_in(key_of[3], 1), 0 - (2 * PIX) // 3, PIX - 1).astype(jnp.int32)
    conv_weight = noise(key_of[4], (27, GROUPS, GROUPS), (27 * GROUPS) ** -0.5, 0.4375)
    return dict(features=features, view_lists=view_lists, requests=requests, warp_idx=warp_idx, conv_weight=conv_weight)


def reference(features, view_lists, requests, warp_idx, conv_weight):
    views = features.shape[0]
    owner_dev = view_lists // CAP
    slot_index = view_lists % CAP
    asker = (jnp.arange(views, dtype=jnp.int32) // VIEW_DEV).astype(jnp.int32)[:, None]
    source = (owner_dev * VIEW_DEV + requests[asker, owner_dev, slot_index]).astype(jnp.int32)
    flat_pool = features.reshape(views * PIX, CHANNELS)

    def one_view(item):
        own_tile, warp_rows, source_ids = item
        usable = warp_rows >= 0
        picks = (source_ids[:, None, None, None] * PIX + jnp.maximum(warp_rows, 0)).astype(jnp.int32)
        warped = jnp.take(flat_pool, picks.reshape(-1), axis=0)
        warped = warped.reshape(SOURCES, DEPTH, PIX, GROUPS, CHANNELS // GROUPS).astype(jnp.float32)
        own_groups = own_tile.reshape(PIX, GROUPS, CHANNELS // GROUPS).astype(jnp.float32)
        products = jnp.einsum('sdpgk,pgk->sdpg', warped, own_groups)
        usable_flat = usable.reshape(SOURCES, DEPTH, PIX)
        masked = jnp.where(usable_flat[..., None], products, jnp.float32(0.0))
        live_count = jnp.sum(usable_flat.astype(jnp.float32), axis=0)
        corr = 0.5 * jnp.sum(masked, axis=0) / jnp.maximum(live_count, jnp.float32(1.0))[..., None]
        corr = jnp.transpose(corr, (2, 0, 1)).reshape(GROUPS, DEPTH, TILE_H, TILE_W)
        return corr.astype(jnp.bfloat16)

    cost = lax.map(one_view, (features, warp_idx, source))
    padded = jnp.pad(cost, ((0, 0), (0, 0), (1, 1), (1, 1), (1, 1)))
    summed = jnp.zeros((views, GROUPS, DEPTH, TILE_H, TILE_W), jnp.float32)
    for depth_tap in range(3):
        for row_tap in range(3):
            for col_tap in range(3):
                shifted = padded[:, :, depth_tap:depth_tap + DEPTH, row_tap:row_tap + TILE_H, col_tap:col_tap + TILE_W]
                kernel = conv_weight[9 * depth_tap + 3 * row_tap + col_tap].astype(jnp.float32)
                summed = summed + jnp.einsum('vgdhw,gk->vkdhw', shifted.astype(jnp.float32), kernel)
    return summed.astype(jnp.bfloat16)
```

```python
import functools

import jax
import jax.numpy as jnp
import numpy as np
from jax import lax
from jax.experimental import pallas as pl
from jax.experimental.pallas import tpu as pltpu
from jax.sharding import PartitionSpec as P

LOW = 256


def cost_kernel(sources, high, kinds, groups, source_ref, idx_ref, pool_ref, own_ref, out_ref):
    view = pl.program_id(0)
    columns = idx_ref.shape[-1]
    pairs = idx_ref.shape[2] // 2
    chans = kinds * groups
    iota = lax.broadcasted_iota(jnp.int32, (16, columns), 0).astype(jnp.float32)
    one = jnp.ones((16, columns), jnp.bfloat16)
    zero = jnp.zeros((16, columns), jnp.bfloat16)
    steps = [(iota + float(16 * m)).astype(jnp.bfloat16) for m in range(LOW // 16)]

    def one_pair(pair, carry):
        total = [jnp.zeros((groups, columns), jnp.float32) for _ in range(2)]
        live = [jnp.zeros((groups, columns), jnp.float32) for _ in range(2)]
        for k in range(sources):
            hots, highs = [], []
            for q in range(2):
                row = idx_ref[0, k, pl.ds(2 * pair + q, 1), :]
                row = jnp.broadcast_to(row, (groups, columns))
                usable = row >= 0
                live[q] = live[q] + jnp.where(usable, 1.0, 0.0)
                low = jnp.where(usable, row & (LOW - 1), -1).astype(jnp.float32)
                low = jnp.concatenate([low, low], axis=0).astype(jnp.bfloat16)
                hots.append(
                    jnp.concatenate([jnp.where(s == low, one, zero) for s in steps], axis=0)
                )
                highs.append(row)
            table = pool_ref[source_ref[view * sources + k]]
            found = jnp.dot(
                table, jnp.concatenate(hots, axis=1), preferred_element_type=jnp.float32
            )
            for q in range(2):
                bits = []
                width = LOW
                while width < LOW * high:
                    bits.append((highs[q] & width) != 0)
                    width *= 2
                for t in range(kinds):
                    parts = [
                        found[
                            h * chans + t * groups : h * chans + (t + 1) * groups,
                            q * columns : (q + 1) * columns,
                        ]
                        for h in range(high)
                    ]
                    for bit in bits:
                        parts = [
                            jnp.where(bit, parts[2 * i + 1], parts[2 * i])
                            for i in range(len(parts) // 2)
                        ]
                    own = own_ref[0, t * groups : (t + 1) * groups, q * columns : (q + 1) * columns]
                    total[q] = total[q] + parts[0] * own
        cost = [0.5 * total[q] / jnp.maximum(live[q], 1.0) for q in range(2)]
        start = pl.multiple_of(pair * 2 * groups, 2 * groups)
        out_ref[0, pl.ds(start, 2 * groups), :] = jnp.concatenate(cost, axis=0).astype(jnp.bfloat16)
        return carry

    lax.fori_loop(0, pairs, one_pair, 0)


def conv_kernel(planes, groups, rows, slab_ref, band_ref, out_ref):
    shares = slab_ref.shape[0]
    columns = slab_ref.shape[-1]
    height = slab_ref.shape[2] // (planes + 2)
    out_rows = groups * rows
    lane = lax.broadcasted_iota(jnp.int32, (out_rows, columns), 1)
    for first in range(0, planes, 2):
        block = jnp.concatenate(
            [
                jnp.concatenate(
                    [slab_ref[s, 0, p * height : (p + 3) * height, :] for s in range(shares)],
                    axis=0,
                )
                for p in (first, first + 1)
            ],
            axis=1,
        )
        mixed = jnp.dot(band_ref[...], block, preferred_element_type=jnp.float32)
        for q in range(2):
            part = mixed[:, q * columns : (q + 1) * columns]
            left = pltpu.roll(part[:out_rows], 1, 1)
            right = pltpu.roll(part[2 * out_rows :], columns - 1, 1)
            total = part[out_rows : 2 * out_rows]
            total = total + jnp.where(lane == 0, 0.0, left)
            total = total + jnp.where(lane == columns - 1, 0.0, right)
            total = total.astype(jnp.bfloat16)
            for h in range(groups):
                out_ref[0, h, first + q] = total[h * rows : (h + 1) * rows]


def on_device(features, view_lists, requests, warp_idx, conv_weight):
    view_here = lax.axis_index("view")
    depth_here = lax.axis_index("depth")
    view_count = lax.axis_size("view")
    depth_count = lax.axis_size("depth")
    views, pixels, channels = features.shape
    sources, planes, row_count, columns = warp_idx.shape[1:]
    groups = conv_weight.shape[1]
    kinds = channels // groups
    high = pixels // LOW
    asked = requests.shape[2]
    rows = row_count * depth_count

    tables = features.reshape(views, high, LOW, groups, kinds).transpose(0, 1, 4, 3, 2)
    tables = tables.reshape(views, high * channels, LOW)
    wanted = requests[:, view_here, :].reshape(-1)
    outgoing = jnp.take(tables, wanted, axis=0).reshape(view_count, asked, high * channels, LOW)
    pool = lax.all_to_all(outgoing, "view", split_axis=0, concat_axis=0, tiled=True)
    pool = pool.reshape(view_count * asked, high * channels, LOW)

    own_pixels = row_count * columns
    own = lax.dynamic_slice_in_dim(features, depth_here * own_pixels, own_pixels, 1)
    own = own.reshape(views, own_pixels, groups, kinds).transpose(0, 3, 2, 1)
    own = own.reshape(views, channels, own_pixels).astype(jnp.float32)
    if row_count == 1:
        own = jnp.concatenate([own, own], axis=2)
    idx = warp_idx.reshape(views, sources, planes * row_count, columns)

    cost = pl.pallas_call(
        functools.partial(cost_kernel, sources, high, kinds, groups),
        grid_spec=pltpu.PrefetchScalarGridSpec(
            num_scalar_prefetch=1,
            grid=(views,),
            in_specs=[
                pl.BlockSpec((1, sources, planes * row_count, columns), lambda v, s: (v, 0, 0, 0)),
                pl.BlockSpec(pool.shape, lambda v, s: (0, 0, 0)),
                pl.BlockSpec((1,) + own.shape[1:], lambda v, s: (v, 0, 0)),
            ],
            out_specs=pl.BlockSpec(
                (1, planes * row_count * groups, columns), lambda v, s: (v, 0, 0)
            ),
        ),
        out_shape=jax.ShapeDtypeStruct(
            (views, planes * row_count * groups, columns), jnp.bfloat16
        ),
        compiler_params=pltpu.CompilerParams(vmem_limit_bytes=40 * 1024 * 1024),
    )(view_lists.reshape(-1), idx, pool, own)

    height = row_count * groups
    slab_planes = planes // depth_count
    padded = jnp.pad(cost, ((0, 0), (height, height), (0, 0)))
    slabs = jnp.stack(
        [
            lax.slice_in_dim(
                padded, t * slab_planes * height, ((t + 1) * slab_planes + 2) * height, axis=1
            )
            for t in range(depth_count)
        ]
    )
    slabs = lax.all_to_all(slabs, "depth", split_axis=0, concat_axis=0, tiled=True)

    place = np.zeros((rows, depth_count, row_count, 3), np.float32)
    for i in range(rows):
        for b in range(3):
            j = i + b - 1
            if 0 <= j < rows:
                place[i, j // row_count, j % row_count, b] = 1.0
    taps = conv_weight.reshape(3, 3, 3, groups, groups)
    band = jnp.einsum(
        "abegh,isrb->ehisarg",
        taps,
        jnp.asarray(place, jnp.bfloat16),
        preferred_element_type=jnp.float32,
    ).astype(jnp.bfloat16)
    band = band.reshape(3 * groups * rows, depth_count * 3 * height)

    return pl.pallas_call(
        functools.partial(conv_kernel, slab_planes, groups, rows),
        grid=(views,),
        in_specs=[
            pl.BlockSpec(
                (depth_count, 1, (slab_planes + 2) * height, columns), lambda v: (0, v, 0, 0)
            ),
            pl.BlockSpec(band.shape, lambda v: (0, 0)),
        ],
        out_specs=pl.BlockSpec(
            (1, groups, slab_planes, rows, columns), lambda v: (v, 0, 0, 0, 0)
        ),
        out_shape=jax.ShapeDtypeStruct(
            (views, groups, slab_planes, rows, columns), jnp.bfloat16
        ),
        compiler_params=pltpu.CompilerParams(vmem_limit_bytes=32 * 1024 * 1024),
    )(slabs, band)


def solution(mesh):
    return jax.shard_map(
        on_device,
        mesh=mesh,
        in_specs=(
            P("view", None, None),
            P("view", None),
            P(),
            P("view", None, None, "depth", None),
            P(),
        ),
        out_specs=P("view", None, "depth", None, None),
        check_vma=False,
    )
```

```python
import functools

import jax
import jax.numpy as jnp
import numpy as np
from jax import lax
from jax.experimental import pallas as pl
from jax.experimental.pallas import tpu as pltpu
from jax.sharding import PartitionSpec as P

LOW = 256


def fetch_kernel(
    asked, ask_ref, tiles_ref, order_ref, pool_ref, stage, send_v, recv_v, send_x, recv_x, send_c, recv_c
):
    views = lax.axis_size("view")
    shares = lax.axis_size("depth")
    lines = shares // 2
    view = lax.axis_index("view")
    depth = lax.axis_index("depth")
    line, core = depth // 2, depth % 2
    other = line * 2 + 1 - core
    width = stage.shape[-1]

    def at_view(step):
        return lax.rem(view + step + views, views)

    def at_line(step):
        return lax.rem(line + step + lines, lines) * 2 + core

    def slots(owner):
        return pl.ds(owner * asked, asked)

    def copy(src, dst, send, recv, where):
        return pltpu.make_async_remote_copy(
            src_ref=src,
            dst_ref=dst,
            send_sem=send,
            recv_sem=recv,
            device_id=where,
            device_id_type=pl.DeviceIdType.MESH,
        )

    barrier = pltpu.get_barrier_semaphore()
    peers = [(at_view(o), depth) for o in range(1, views)]
    peers += [(view, at_line(o)) for o in range(1, lines)]
    peers += [(view, other)]
    for peer in peers:
        pl.semaphore_signal(barrier, inc=1, device_id=peer, device_id_type=pl.DeviceIdType.MESH)

    start = pl.multiple_of(depth * width, width)
    for owner in range(views):
        for c in range(asked):
            tile = tiles_ref[ask_ref[(owner * views + view) * asked + c], :, pl.ds(start, width)]
            moved = jnp.dot(order_ref[...], tile, preferred_element_type=jnp.float32)
            stage[owner, c] = moved.astype(jnp.bfloat16)
    pl.semaphore_wait(barrier, len(peers))

    over_view = []
    for o in range(1, views):
        step = copy(
            stage.at[at_view(o)],
            pool_ref.at[depth, slots(view)],
            send_v.at[o - 1],
            recv_v.at[o - 1],
            (at_view(o), depth),
        )
        step.start()
        over_view.append(step)
    pool_ref[depth, slots(view)] = stage[view]

    over_line, over_core = [], []
    for o in range(views):
        mine = pool_ref.at[depth, slots(at_view(-o))]
        if o > 0:
            copy(
                stage.at[at_view(o)], mine, send_v.at[o - 1], recv_v.at[o - 1], (at_view(o), depth)
            ).wait_recv()
        for x in range(1, lines):
            step = copy(
                mine, mine, send_x.at[x - 1, o], recv_x.at[x - 1, o], (view, at_line(x))
            )
            step.start()
            over_line.append(step)
        step = copy(mine, mine, send_c.at[0, o], recv_c.at[0, o], (view, other))
        step.start()
        over_core.append(step)
    for o in range(views):
        for x in range(1, lines):
            theirs = pool_ref.at[at_line(-x), slots(at_view(-o))]
            copy(
                theirs, theirs, send_x.at[x - 1, o], recv_x.at[x - 1, o], (view, at_line(x))
            ).wait_recv()
            step = copy(theirs, theirs, send_c.at[x, o], recv_c.at[x, o], (view, other))
            step.start()
            over_core.append(step)
    for o in range(views):
        for x in range(lines):
            share = lax.rem(line - x + lines, lines) * 2 + 1 - core
            there = pool_ref.at[share, slots(at_view(-o))]
            copy(there, there, send_c.at[x, o], recv_c.at[x, o], (view, other)).wait_recv()
    for step in over_view + over_line + over_core:
        step.wait_send()


def cost_kernel(
    sources, high, kinds, groups, source_ref, idx_ref, pool_ref, own_ref, out_ref, low_ref, scale_ref
):
    view = pl.program_id(0)
    columns = idx_ref.shape[-1]
    pairs = idx_ref.shape[2] // 2
    chans = kinds * groups
    per = pool_ref.shape[0] // high
    iota = lax.broadcasted_iota(jnp.int32, (16, columns), 0).astype(jnp.float32)
    one = jnp.ones((16, columns), jnp.bfloat16)
    zero = jnp.zeros((16, columns), jnp.bfloat16)
    steps = [(iota + float(16 * m)).astype(jnp.bfloat16) for m in range(LOW // 16)]

    live = jnp.zeros(scale_ref.shape, jnp.float32)
    for k in range(sources):
        usable = idx_ref[0, k] >= 0
        low_ref[k] = jnp.where(usable, idx_ref[0, k] & (LOW - 1), -1).astype(jnp.float32)
        live = live + jnp.where(usable, 1.0, 0.0)
    scale_ref[...] = 0.5 / jnp.maximum(live, 1.0)

    def one_pair(pair, carry):
        total = [[None] * kinds for _ in range(2)]
        for k in range(sources):
            hots, highs = [], []
            for q in range(2):
                row = idx_ref[0, k, pl.ds(2 * pair + q, 1), :]
                highs.append(jnp.broadcast_to(row, (groups, columns)))
                low = low_ref[k, pl.ds(2 * pair + q, 1), :]
                low = jnp.broadcast_to(low, (16, columns)).astype(jnp.bfloat16)
                hots.append(
                    jnp.concatenate([jnp.where(s == low, one, zero) for s in steps], axis=0)
                )
            source = source_ref[view * sources + k]
            table = jnp.concatenate(
                [
                    jnp.concatenate(
                        [pool_ref[h * per + i, source] for i in range(per)], axis=1
                    )
                    for h in range(high)
                ],
                axis=0,
            )
            found = jnp.dot(
                table, jnp.concatenate(hots, axis=1), preferred_element_type=jnp.float32
            )
            for q in range(2):
                bits = []
                width = LOW
                while width < LOW * high:
                    bits.append((highs[q] & width) != 0)
                    width *= 2
                for t in range(kinds):
                    parts = [
                        found[
                            h * chans + t * groups : h * chans + (t + 1) * groups,
                            q * columns : (q + 1) * columns,
                        ]
                        for h in range(high)
                    ]
                    for bit in bits:
                        parts = [
                            jnp.where(bit, parts[2 * i + 1], parts[2 * i])
                            for i in range(len(parts) // 2)
                        ]
                    total[q][t] = parts[0] if k == 0 else total[q][t] + parts[0]
        cost = []
        for q in range(2):
            summed = None
            for t in range(kinds):
                own = own_ref[0, t * groups : (t + 1) * groups, q * columns : (q + 1) * columns]
                term = total[q][t] * own
                summed = term if summed is None else summed + term
            cost.append(summed * scale_ref[pl.ds(2 * pair + q, 1), :])
        start = pl.multiple_of(pair * 2 * groups, 2 * groups)
        out_ref[0, pl.ds(start, 2 * groups), :] = jnp.concatenate(cost, axis=0).astype(jnp.bfloat16)
        return carry

    lax.fori_loop(0, pairs, one_pair, 0)


def conv_kernel(planes, groups, rows, slab_ref, band_ref, out_ref):
    shares = slab_ref.shape[0]
    columns = slab_ref.shape[-1]
    height = slab_ref.shape[2] // (planes + 2)
    out_rows = groups * rows
    lane = lax.broadcasted_iota(jnp.int32, (out_rows, columns), 1)
    for first in range(0, planes, 2):
        block = jnp.concatenate(
            [
                jnp.concatenate(
                    [slab_ref[s, 0, p * height : (p + 3) * height, :] for s in range(shares)],
                    axis=0,
                )
                for p in (first, first + 1)
            ],
            axis=1,
        )
        mixed = jnp.dot(band_ref[...], block, preferred_element_type=jnp.float32)
        for q in range(2):
            part = mixed[:, q * columns : (q + 1) * columns]
            left = pltpu.roll(part[:out_rows], 1, 1)
            right = pltpu.roll(part[2 * out_rows :], columns - 1, 1)
            total = part[out_rows : 2 * out_rows]
            total = total + jnp.where(lane == 0, 0.0, left)
            total = total + jnp.where(lane == columns - 1, 0.0, right)
            total = total.astype(jnp.bfloat16)
            for h in range(groups):
                out_ref[0, h, first + q] = total[h * rows : (h + 1) * rows]


def on_device(features, view_lists, requests, warp_idx, conv_weight):
    depth_here = lax.axis_index("depth")
    view_count = lax.axis_size("view")
    depth_count = lax.axis_size("depth")
    views, pixels, channels = features.shape
    sources, planes, row_count, columns = warp_idx.shape[1:]
    groups = conv_weight.shape[1]
    kinds = channels // groups
    high = pixels // LOW
    asked = requests.shape[2]
    rows = row_count * depth_count

    lines = depth_count // 2
    share = pixels // depth_count
    order = np.zeros((channels, channels), np.float32)
    for c in range(channels):
        order[(c % kinds) * groups + c // kinds, c] = 1.0
    pool = pl.pallas_call(
        functools.partial(fetch_kernel, asked),
        out_shape=jax.ShapeDtypeStruct(
            (depth_count, view_count * asked, channels, share), jnp.bfloat16
        ),
        in_specs=[
            pl.BlockSpec(memory_space=pltpu.SMEM),
            pl.BlockSpec(memory_space=pltpu.VMEM),
            pl.BlockSpec(memory_space=pltpu.VMEM),
        ],
        out_specs=pl.BlockSpec(memory_space=pltpu.VMEM),
        scratch_shapes=[
            pltpu.VMEM((view_count, asked, channels, share), jnp.bfloat16),
            pltpu.SemaphoreType.DMA((view_count - 1,)),
            pltpu.SemaphoreType.DMA((view_count - 1,)),
            pltpu.SemaphoreType.DMA((lines, view_count)),
            pltpu.SemaphoreType.DMA((lines, view_count)),
            pltpu.SemaphoreType.DMA((lines, view_count)),
            pltpu.SemaphoreType.DMA((lines, view_count)),
        ],
        compiler_params=pltpu.CompilerParams(
            collective_id=0, has_side_effects=True, vmem_limit_bytes=16 * 1024 * 1024
        ),
    )(requests.reshape(-1), features.transpose(0, 2, 1), jnp.asarray(order, jnp.bfloat16))

    own_pixels = row_count * columns
    own = lax.dynamic_slice_in_dim(features, depth_here * own_pixels, own_pixels, 1)
    own = own.reshape(views, own_pixels, groups, kinds).transpose(0, 3, 2, 1)
    own = own.reshape(views, channels, own_pixels).astype(jnp.float32)
    if row_count == 1:
        own = jnp.concatenate([own, own], axis=2)
    idx = warp_idx.reshape(views, sources, planes * row_count, columns)

    cost = pl.pallas_call(
        functools.partial(cost_kernel, sources, high, kinds, groups),
        grid_spec=pltpu.PrefetchScalarGridSpec(
            num_scalar_prefetch=1,
            grid=(views,),
            in_specs=[
                pl.BlockSpec((1, sources, planes * row_count, columns), lambda v, s: (v, 0, 0, 0)),
                pl.BlockSpec(pool.shape, lambda v, s: (0, 0, 0, 0)),
                pl.BlockSpec((1,) + own.shape[1:], lambda v, s: (v, 0, 0)),
            ],
            out_specs=pl.BlockSpec(
                (1, planes * row_count * groups, columns), lambda v, s: (v, 0, 0)
            ),
            scratch_shapes=[
                pltpu.VMEM((sources, planes * row_count, columns), jnp.float32),
                pltpu.VMEM((planes * row_count, columns), jnp.float32),
            ],
        ),
        out_shape=jax.ShapeDtypeStruct(
            (views, planes * row_count * groups, columns), jnp.bfloat16
        ),
        compiler_params=pltpu.CompilerParams(vmem_limit_bytes=40 * 1024 * 1024),
    )(view_lists.reshape(-1), idx, pool, own)

    height = row_count * groups
    slab_planes = planes // depth_count
    padded = jnp.pad(cost, ((0, 0), (height, height), (0, 0)))
    slabs = jnp.stack(
        [
            lax.slice_in_dim(
                padded, t * slab_planes * height, ((t + 1) * slab_planes + 2) * height, axis=1
            )
            for t in range(depth_count)
        ]
    )
    slabs = lax.all_to_all(slabs, "depth", split_axis=0, concat_axis=0, tiled=True)

    place = np.zeros((rows, depth_count, row_count, 3), np.float32)
    for i in range(rows):
        for b in range(3):
            j = i + b - 1
            if 0 <= j < rows:
                place[i, j // row_count, j % row_count, b] = 1.0
    taps = conv_weight.reshape(3, 3, 3, groups, groups)
    band = jnp.einsum(
        "abegh,isrb->ehisarg",
        taps,
        jnp.asarray(place, jnp.bfloat16),
        preferred_element_type=jnp.float32,
    ).astype(jnp.bfloat16)
    band = band.reshape(3 * groups * rows, depth_count * 3 * height)

    return pl.pallas_call(
        functools.partial(conv_kernel, slab_planes, groups, rows),
        grid=(views,),
        in_specs=[
            pl.BlockSpec(
                (depth_count, 1, (slab_planes + 2) * height, columns), lambda v: (0, v, 0, 0)
            ),
            pl.BlockSpec(band.shape, lambda v: (0, 0)),
        ],
        out_specs=pl.BlockSpec(
            (1, groups, slab_planes, rows, columns), lambda v: (v, 0, 0, 0, 0)
        ),
        out_shape=jax.ShapeDtypeStruct(
            (views, groups, slab_planes, rows, columns), jnp.bfloat16
        ),
        compiler_params=pltpu.CompilerParams(vmem_limit_bytes=32 * 1024 * 1024),
    )(slabs, band)


def solution(mesh):
    return jax.shard_map(
        on_device,
        mesh=mesh,
        in_specs=(
            P("view", None, None),
            P("view", None),
            P(),
            P("view", None, None, "depth", None),
            P(),
        ),
        out_specs=P("view", None, "depth", None, None),
        check_vma=False,
    )
```

```python
import functools

import jax
import jax.numpy as jnp
import numpy as np
from jax import lax
from jax.experimental import pallas as pl
from jax.experimental.pallas import tpu as pltpu
from jax.sharding import PartitionSpec as P

LOW = 128


def fetch_kernel(
    asked, ask_ref, tiles_ref, order_ref, pool_ref, stage, send_v, recv_v, send_x, recv_x, send_c, recv_c
):
    views = lax.axis_size("view")
    shares = lax.axis_size("depth")
    lines = shares // 2
    view = lax.axis_index("view")
    depth = lax.axis_index("depth")
    line, core = depth // 2, depth % 2
    other = line * 2 + 1 - core
    width = stage.shape[-1]

    def at_view(step):
        return lax.rem(view + step + views, views)

    def at_line(step):
        return lax.rem(line + step + lines, lines) * 2 + core

    def slots(owner):
        return pl.ds(owner * asked, asked)

    def copy(src, dst, send, recv, where):
        return pltpu.make_async_remote_copy(
            src_ref=src,
            dst_ref=dst,
            send_sem=send,
            recv_sem=recv,
            device_id=where,
            device_id_type=pl.DeviceIdType.MESH,
        )

    barrier = pltpu.get_barrier_semaphore()
    peers = [(at_view(o), depth) for o in range(1, views)]
    peers += [(view, at_line(o)) for o in range(1, lines)]
    peers += [(view, other)]
    for peer in peers:
        pl.semaphore_signal(barrier, inc=1, device_id=peer, device_id_type=pl.DeviceIdType.MESH)

    start = pl.multiple_of(depth * width, width)
    for owner in range(views):
        for c in range(asked):
            tile = tiles_ref[ask_ref[(owner * views + view) * asked + c], :, pl.ds(start, width)]
            moved = jnp.dot(order_ref[...], tile, preferred_element_type=jnp.float32)
            stage[owner, c] = moved.astype(jnp.bfloat16)
    pl.semaphore_wait(barrier, len(peers))

    over_view = []
    for o in range(1, views):
        step = copy(
            stage.at[at_view(o)],
            pool_ref.at[depth, slots(view)],
            send_v.at[o - 1],
            recv_v.at[o - 1],
            (at_view(o), depth),
        )
        step.start()
        over_view.append(step)
    pool_ref[depth, slots(view)] = stage[view]

    over_line, over_core = [], []
    for o in range(views):
        mine = pool_ref.at[depth, slots(at_view(-o))]
        if o > 0:
            copy(
                stage.at[at_view(o)], mine, send_v.at[o - 1], recv_v.at[o - 1], (at_view(o), depth)
            ).wait_recv()
        for x in range(1, lines):
            step = copy(
                mine, mine, send_x.at[x - 1, o], recv_x.at[x - 1, o], (view, at_line(x))
            )
            step.start()
            over_line.append(step)
        step = copy(mine, mine, send_c.at[0, o], recv_c.at[0, o], (view, other))
        step.start()
        over_core.append(step)
    for o in range(views):
        for x in range(1, lines):
            theirs = pool_ref.at[at_line(-x), slots(at_view(-o))]
            copy(
                theirs, theirs, send_x.at[x - 1, o], recv_x.at[x - 1, o], (view, at_line(x))
            ).wait_recv()
            step = copy(theirs, theirs, send_c.at[x, o], recv_c.at[x, o], (view, other))
            step.start()
            over_core.append(step)
    for o in range(views):
        for x in range(lines):
            share = lax.rem(line - x + lines, lines) * 2 + 1 - core
            there = pool_ref.at[share, slots(at_view(-o))]
            copy(there, there, send_c.at[x, o], recv_c.at[x, o], (view, other)).wait_recv()
    for step in over_view + over_line + over_core:
        step.wait_send()


def cost_kernel(
    sources, high, kinds, groups, source_ref, idx_ref, pool_ref, own_ref, out_ref, low_ref, scale_ref
):
    view = pl.program_id(0)
    columns = idx_ref.shape[-1]
    pairs = idx_ref.shape[2] // 2
    chans = kinds * groups
    share = pool_ref.shape[-1]
    iota = lax.broadcasted_iota(jnp.int32, (16, columns), 0).astype(jnp.float32)
    one = jnp.ones((16, columns), jnp.bfloat16)
    zero = jnp.zeros((16, columns), jnp.bfloat16)
    steps = [(iota + float(16 * m)).astype(jnp.bfloat16) for m in range(LOW // 16)]

    live = jnp.zeros(scale_ref.shape, jnp.float32)
    for k in range(sources):
        usable = idx_ref[0, k] >= 0
        low_ref[k] = jnp.where(usable, idx_ref[0, k] & (LOW - 1), -1).astype(jnp.float32)
        live = live + jnp.where(usable, 1.0, 0.0)
    scale_ref[...] = 0.5 / jnp.maximum(live, 1.0)

    def one_pair(pair, carry):
        total = [[None] * kinds for _ in range(2)]
        for k in range(sources):
            hots, highs = [], []
            for q in range(2):
                row = idx_ref[0, k, pl.ds(2 * pair + q, 1), :]
                highs.append(jnp.broadcast_to(row, (groups, columns)))
                low = low_ref[k, pl.ds(2 * pair + q, 1), :]
                low = jnp.broadcast_to(low, (16, columns)).astype(jnp.bfloat16)
                hots.append(
                    jnp.concatenate([jnp.where(s == low, one, zero) for s in steps], axis=0)
                )
            source = source_ref[view * sources + k]
            table = jnp.concatenate(
                [
                    pool_ref[h * LOW // share, source, :, h * LOW % share : h * LOW % share + LOW]
                    for h in range(high)
                ],
                axis=0,
            )
            found = jnp.dot(
                table, jnp.concatenate(hots, axis=1), preferred_element_type=jnp.float32
            )
            for q in range(2):
                bits = []
                width = LOW
                while width < LOW * high:
                    bits.append((highs[q] & width) != 0)
                    width *= 2
                for t in range(kinds):
                    parts = [
                        found[
                            h * chans + t * groups : h * chans + (t + 1) * groups,
                            q * columns : (q + 1) * columns,
                        ]
                        for h in range(high)
                    ]
                    for bit in bits:
                        parts = [
                            jnp.where(bit, parts[2 * i + 1], parts[2 * i])
                            for i in range(len(parts) // 2)
                        ]
                    total[q][t] = parts[0] if k == 0 else total[q][t] + parts[0]
        cost = []
        for q in range(2):
            summed = None
            for t in range(kinds):
                own = own_ref[0, t * groups : (t + 1) * groups, q * columns : (q + 1) * columns]
                term = total[q][t] * own
                summed = term if summed is None else summed + term
            cost.append(summed * scale_ref[pl.ds(2 * pair + q, 1), :])
        start = pl.multiple_of(pair * 2 * groups, 2 * groups)
        out_ref[0, pl.ds(start, 2 * groups), :] = jnp.concatenate(cost, axis=0).astype(jnp.bfloat16)
        return carry

    lax.fori_loop(0, pairs, one_pair, 0)


def conv_kernel(planes, groups, rows, slab_ref, band_ref, out_ref):
    shares = slab_ref.shape[0]
    columns = slab_ref.shape[-1]
    height = slab_ref.shape[2] // (planes + 2)
    out_rows = groups * rows
    lane = lax.broadcasted_iota(jnp.int32, (out_rows, columns), 1)
    for first in range(0, planes, 2):
        block = jnp.concatenate(
            [
                jnp.concatenate(
                    [slab_ref[s, 0, p * height : (p + 3) * height, :] for s in range(shares)],
                    axis=0,
                )
                for p in (first, first + 1)
            ],
            axis=1,
        )
        mixed = jnp.dot(band_ref[...], block, preferred_element_type=jnp.float32)
        for q in range(2):
            part = mixed[:, q * columns : (q + 1) * columns]
            left = pltpu.roll(part[:out_rows], 1, 1)
            right = pltpu.roll(part[2 * out_rows :], columns - 1, 1)
            total = part[out_rows : 2 * out_rows]
            total = total + jnp.where(lane == 0, 0.0, left)
            total = total + jnp.where(lane == columns - 1, 0.0, right)
            total = total.astype(jnp.bfloat16)
            for h in range(groups):
                out_ref[0, h, first + q] = total[h * rows : (h + 1) * rows]


def on_device(features, view_lists, requests, warp_idx, conv_weight):
    depth_here = lax.axis_index("depth")
    view_count = lax.axis_size("view")
    depth_count = lax.axis_size("depth")
    views, pixels, channels = features.shape
    sources, planes, row_count, columns = warp_idx.shape[1:]
    groups = conv_weight.shape[1]
    kinds = channels // groups
    high = pixels // LOW
    asked = requests.shape[2]
    rows = row_count * depth_count

    lines = depth_count // 2
    share = pixels // depth_count
    order = np.zeros((channels, channels), np.float32)
    for c in range(channels):
        order[(c % kinds) * groups + c // kinds, c] = 1.0
    pool = pl.pallas_call(
        functools.partial(fetch_kernel, asked),
        out_shape=jax.ShapeDtypeStruct(
            (depth_count, view_count * asked, channels, share), jnp.bfloat16
        ),
        in_specs=[
            pl.BlockSpec(memory_space=pltpu.SMEM),
            pl.BlockSpec(memory_space=pltpu.VMEM),
            pl.BlockSpec(memory_space=pltpu.VMEM),
        ],
        out_specs=pl.BlockSpec(memory_space=pltpu.VMEM),
        scratch_shapes=[
            pltpu.VMEM((view_count, asked, channels, share), jnp.bfloat16),
            pltpu.SemaphoreType.DMA((view_count - 1,)),
            pltpu.SemaphoreType.DMA((view_count - 1,)),
            pltpu.SemaphoreType.DMA((lines, view_count)),
            pltpu.SemaphoreType.DMA((lines, view_count)),
            pltpu.SemaphoreType.DMA((lines, view_count)),
            pltpu.SemaphoreType.DMA((lines, view_count)),
        ],
        compiler_params=pltpu.CompilerParams(
            collective_id=0, has_side_effects=True, vmem_limit_bytes=16 * 1024 * 1024
        ),
    )(requests.reshape(-1), features.transpose(0, 2, 1), jnp.asarray(order, jnp.bfloat16))

    own_pixels = row_count * columns
    own = lax.dynamic_slice_in_dim(features, depth_here * own_pixels, own_pixels, 1)
    own = own.reshape(views, own_pixels, groups, kinds).transpose(0, 3, 2, 1)
    own = own.reshape(views, channels, own_pixels).astype(jnp.float32)
    if row_count == 1:
        own = jnp.concatenate([own, own], axis=2)
    idx = warp_idx.reshape(views, sources, planes * row_count, columns)

    cost = pl.pallas_call(
        functools.partial(cost_kernel, sources, high, kinds, groups),
        grid_spec=pltpu.PrefetchScalarGridSpec(
            num_scalar_prefetch=1,
            grid=(views,),
            in_specs=[
                pl.BlockSpec((1, sources, planes * row_count, columns), lambda v, s: (v, 0, 0, 0)),
                pl.BlockSpec(pool.shape, lambda v, s: (0, 0, 0, 0)),
                pl.BlockSpec((1,) + own.shape[1:], lambda v, s: (v, 0, 0)),
            ],
            out_specs=pl.BlockSpec(
                (1, planes * row_count * groups, columns), lambda v, s: (v, 0, 0)
            ),
            scratch_shapes=[
                pltpu.VMEM((sources, planes * row_count, columns), jnp.float32),
                pltpu.VMEM((planes * row_count, columns), jnp.float32),
            ],
        ),
        out_shape=jax.ShapeDtypeStruct(
            (views, planes * row_count * groups, columns), jnp.bfloat16
        ),
        compiler_params=pltpu.CompilerParams(vmem_limit_bytes=40 * 1024 * 1024),
    )(view_lists.reshape(-1), idx, pool, own)

    height = row_count * groups
    slab_planes = planes // depth_count
    padded = jnp.pad(cost, ((0, 0), (height, height), (0, 0)))
    slabs = jnp.stack(
        [
            lax.slice_in_dim(
                padded, t * slab_planes * height, ((t + 1) * slab_planes + 2) * height, axis=1
            )
            for t in range(depth_count)
        ]
    )
    slabs = lax.all_to_all(slabs, "depth", split_axis=0, concat_axis=0, tiled=True)

    place = np.zeros((rows, depth_count, row_count, 3), np.float32)
    for i in range(rows):
        for b in range(3):
            j = i + b - 1
            if 0 <= j < rows:
                place[i, j // row_count, j % row_count, b] = 1.0
    taps = conv_weight.reshape(3, 3, 3, groups, groups)
    band = jnp.einsum(
        "abegh,isrb->ehisarg",
        taps,
        jnp.asarray(place, jnp.bfloat16),
        preferred_element_type=jnp.float32,
    ).astype(jnp.bfloat16)
    band = band.reshape(3 * groups * rows, depth_count * 3 * height)

    return pl.pallas_call(
        functools.partial(conv_kernel, slab_planes, groups, rows),
        grid=(views,),
        in_specs=[
            pl.BlockSpec(
                (depth_count, 1, (slab_planes + 2) * height, columns), lambda v: (0, v, 0, 0)
            ),
            pl.BlockSpec(band.shape, lambda v: (0, 0)),
        ],
        out_specs=pl.BlockSpec(
            (1, groups, slab_planes, rows, columns), lambda v: (v, 0, 0, 0, 0)
        ),
        out_shape=jax.ShapeDtypeStruct(
            (views, groups, slab_planes, rows, columns), jnp.bfloat16
        ),
        compiler_params=pltpu.CompilerParams(vmem_limit_bytes=32 * 1024 * 1024),
    )(slabs, band)


def solution(mesh):
    return jax.shard_map(
        on_device,
        mesh=mesh,
        in_specs=(
            P("view", None, None),
            P("view", None),
            P(),
            P("view", None, None, "depth", None),
            P(),
        ),
        out_specs=P("view", None, "depth", None, None),
        check_vma=False,
    )
```

```python
import functools

import jax
import jax.numpy as jnp
import numpy as np
from jax import lax
from jax.experimental import pallas as pl
from jax.experimental.pallas import tpu as pltpu
from jax.sharding import PartitionSpec as P

LOW = 256


def fetch_kernel(
    asked, ask_ref, tiles_ref, order_ref, pool_ref, stage, send_v, recv_v, send_x, recv_x, send_c, recv_c
):
    views = lax.axis_size("view")
    shares = lax.axis_size("depth")
    lines = shares // 2
    view = lax.axis_index("view")
    depth = lax.axis_index("depth")
    line, core = depth // 2, depth % 2
    other = line * 2 + 1 - core
    width = stage.shape[-1]

    def at_view(step):
        return lax.rem(view + step + views, views)

    def at_line(step):
        return lax.rem(line + step + lines, lines) * 2 + core

    def slots(owner):
        return pl.ds(owner * asked, asked)

    def copy(src, dst, send, recv, where):
        return pltpu.make_async_remote_copy(
            src_ref=src,
            dst_ref=dst,
            send_sem=send,
            recv_sem=recv,
            device_id=where,
            device_id_type=pl.DeviceIdType.MESH,
        )

    barrier = pltpu.get_barrier_semaphore()
    peers = [(at_view(o), depth) for o in range(1, views)]
    peers += [(view, at_line(o)) for o in range(1, lines)]
    peers += [(view, other)]
    for peer in peers:
        pl.semaphore_signal(barrier, inc=1, device_id=peer, device_id_type=pl.DeviceIdType.MESH)

    start = pl.multiple_of(depth * width, width)
    for owner in range(views):
        for c in range(asked):
            tile = tiles_ref[ask_ref[(owner * views + view) * asked + c], :, pl.ds(start, width)]
            moved = jnp.dot(order_ref[...], tile, preferred_element_type=jnp.float32)
            stage[owner, c] = moved.astype(jnp.bfloat16)
    pl.semaphore_wait(barrier, len(peers))

    over_view = []
    for o in range(1, views):
        step = copy(
            stage.at[at_view(o)],
            pool_ref.at[depth, slots(view)],
            send_v.at[o - 1],
            recv_v.at[o - 1],
            (at_view(o), depth),
        )
        step.start()
        over_view.append(step)
    pool_ref[depth, slots(view)] = stage[view]

    over_line, over_core = [], []
    for o in range(views):
        mine = pool_ref.at[depth, slots(at_view(-o))]
        if o > 0:
            copy(
                stage.at[at_view(o)], mine, send_v.at[o - 1], recv_v.at[o - 1], (at_view(o), depth)
            ).wait_recv()
        for x in range(1, lines):
            step = copy(
                mine, mine, send_x.at[x - 1, o], recv_x.at[x - 1, o], (view, at_line(x))
            )
            step.start()
            over_line.append(step)
        step = copy(mine, mine, send_c.at[0, o], recv_c.at[0, o], (view, other))
        step.start()
        over_core.append(step)
    for o in range(views):
        for x in range(1, lines):
            theirs = pool_ref.at[at_line(-x), slots(at_view(-o))]
            copy(
                theirs, theirs, send_x.at[x - 1, o], recv_x.at[x - 1, o], (view, at_line(x))
            ).wait_recv()
            step = copy(theirs, theirs, send_c.at[x, o], recv_c.at[x, o], (view, other))
            step.start()
            over_core.append(step)
    for o in range(views):
        for x in range(lines):
            share = lax.rem(line - x + lines, lines) * 2 + 1 - core
            there = pool_ref.at[share, slots(at_view(-o))]
            copy(there, there, send_c.at[x, o], recv_c.at[x, o], (view, other)).wait_recv()
    for step in over_view + over_line + over_core:
        step.wait_send()


def cost_kernel(
    sources, high, kinds, groups, source_ref, idx_ref, pool_ref, own_ref, out_ref, table_ref, low_ref, scale_ref
):
    view = pl.program_id(0)
    columns = idx_ref.shape[-1]
    pairs = idx_ref.shape[2] // 2
    per = pool_ref.shape[0] // high
    iota = lax.broadcasted_iota(jnp.int32, (16, columns), 0).astype(jnp.float32)
    one = jnp.ones((16, columns), jnp.bfloat16)
    zero = jnp.zeros((16, columns), jnp.bfloat16)
    steps = [(iota + float(16 * m)).astype(jnp.bfloat16) for m in range(LOW // 16)]

    @pl.when(view == 0)
    def _():
        for slot in range(pool_ref.shape[1]):
            parts = [
                jnp.concatenate([pool_ref[h * per + i, slot] for i in range(per)], axis=1)
                for h in range(high)
            ]
            parts = [part.astype(jnp.float32) for part in parts]
            table_ref[slot] = jnp.concatenate(
                [
                    parts[h][t * groups : (t + 1) * groups]
                    for t in range(kinds)
                    for h in range(high)
                ],
                axis=0,
            ).astype(jnp.bfloat16)

    live = jnp.zeros(scale_ref.shape, jnp.float32)
    for k in range(sources):
        usable = idx_ref[0, k] >= 0
        low_ref[k] = jnp.where(usable, idx_ref[0, k] & (LOW - 1), -1).astype(jnp.float32)
        live = live + jnp.where(usable, 1.0, 0.0)
    scale_ref[...] = 0.5 / jnp.maximum(live, 1.0)

    def one_pair(pair, carry):
        total = [[None] * kinds for _ in range(2)]
        for k in range(sources):
            hots, highs = [], []
            for q in range(2):
                row = idx_ref[0, k, pl.ds(2 * pair + q, 1), :]
                highs.append(jnp.broadcast_to(row, (groups, columns)))
                low = low_ref[k, pl.ds(2 * pair + q, 1), :]
                low = jnp.broadcast_to(low, (16, columns)).astype(jnp.bfloat16)
                hots.append(
                    jnp.concatenate([jnp.where(s == low, one, zero) for s in steps], axis=0)
                )
            table = table_ref[source_ref[view * sources + k]]
            found = jnp.dot(
                table, jnp.concatenate(hots, axis=1), preferred_element_type=jnp.float32
            )
            for q in range(2):
                bits = []
                width = LOW
                while width < LOW * high:
                    bits.append((highs[q] & width) != 0)
                    width *= 2
                for t in range(kinds):
                    parts = [
                        found[
                            (t * high + h) * groups : (t * high + h + 1) * groups,
                            q * columns : (q + 1) * columns,
                        ]
                        for h in range(high)
                    ]
                    for bit in bits:
                        parts = [
                            jnp.where(bit, parts[2 * i + 1], parts[2 * i])
                            for i in range(len(parts) // 2)
                        ]
                    total[q][t] = parts[0] if k == 0 else total[q][t] + parts[0]
        cost = []
        for q in range(2):
            summed = None
            for t in range(kinds):
                own = own_ref[0, t * groups : (t + 1) * groups, q * columns : (q + 1) * columns]
                term = total[q][t] * own
                summed = term if summed is None else summed + term
            cost.append(summed * scale_ref[pl.ds(2 * pair + q, 1), :])
        start = pl.multiple_of(pair * 2 * groups, 2 * groups)
        out_ref[0, pl.ds(start, 2 * groups), :] = jnp.concatenate(cost, axis=0).astype(jnp.bfloat16)
        return carry

    lax.fori_loop(0, pairs, one_pair, 0)


def conv_kernel(planes, groups, rows, slab_ref, band_ref, out_ref):
    shares = slab_ref.shape[0]
    columns = slab_ref.shape[-1]
    height = slab_ref.shape[2] // (planes + 2)
    out_rows = groups * rows
    lane = lax.broadcasted_iota(jnp.int32, (out_rows, columns), 1)
    for first in range(0, planes, 2):
        block = jnp.concatenate(
            [
                jnp.concatenate(
                    [slab_ref[s, 0, p * height : (p + 3) * height, :] for s in range(shares)],
                    axis=0,
                )
                for p in (first, first + 1)
            ],
            axis=1,
        )
        mixed = jnp.dot(band_ref[...], block, preferred_element_type=jnp.float32)
        for q in range(2):
            part = mixed[:, q * columns : (q + 1) * columns]
            left = pltpu.roll(part[:out_rows], 1, 1)
            right = pltpu.roll(part[2 * out_rows :], columns - 1, 1)
            total = part[out_rows : 2 * out_rows]
            total = total + jnp.where(lane == 0, 0.0, left)
            total = total + jnp.where(lane == columns - 1, 0.0, right)
            total = total.astype(jnp.bfloat16)
            for h in range(groups):
                out_ref[0, h, first + q] = total[h * rows : (h + 1) * rows]


def on_device(features, view_lists, requests, warp_idx, conv_weight):
    depth_here = lax.axis_index("depth")
    view_count = lax.axis_size("view")
    depth_count = lax.axis_size("depth")
    views, pixels, channels = features.shape
    sources, planes, row_count, columns = warp_idx.shape[1:]
    groups = conv_weight.shape[1]
    kinds = channels // groups
    high = pixels // LOW
    asked = requests.shape[2]
    rows = row_count * depth_count

    lines = depth_count // 2
    share = pixels // depth_count
    order = np.zeros((channels, channels), np.float32)
    for c in range(channels):
        order[(c % kinds) * groups + c // kinds, c] = 1.0
    pool = pl.pallas_call(
        functools.partial(fetch_kernel, asked),
        out_shape=jax.ShapeDtypeStruct(
            (depth_count, view_count * asked, channels, share), jnp.bfloat16
        ),
        in_specs=[
            pl.BlockSpec(memory_space=pltpu.SMEM),
            pl.BlockSpec(memory_space=pltpu.VMEM),
            pl.BlockSpec(memory_space=pltpu.VMEM),
        ],
        out_specs=pl.BlockSpec(memory_space=pltpu.VMEM),
        scratch_shapes=[
            pltpu.VMEM((view_count, asked, channels, share), jnp.bfloat16),
            pltpu.SemaphoreType.DMA((view_count - 1,)),
            pltpu.SemaphoreType.DMA((view_count - 1,)),
            pltpu.SemaphoreType.DMA((lines, view_count)),
            pltpu.SemaphoreType.DMA((lines, view_count)),
            pltpu.SemaphoreType.DMA((lines, view_count)),
            pltpu.SemaphoreType.DMA((lines, view_count)),
        ],
        compiler_params=pltpu.CompilerParams(
            collective_id=0, has_side_effects=True, vmem_limit_bytes=16 * 1024 * 1024
        ),
    )(requests.reshape(-1), features.transpose(0, 2, 1), jnp.asarray(order, jnp.bfloat16))

    own_pixels = row_count * columns
    own = lax.dynamic_slice_in_dim(features, depth_here * own_pixels, own_pixels, 1)
    own = own.reshape(views, own_pixels, groups, kinds).transpose(0, 3, 2, 1)
    own = own.reshape(views, channels, own_pixels).astype(jnp.float32)
    if row_count == 1:
        own = jnp.concatenate([own, own], axis=2)
    idx = warp_idx.reshape(views, sources, planes * row_count, columns)

    cost = pl.pallas_call(
        functools.partial(cost_kernel, sources, high, kinds, groups),
        grid_spec=pltpu.PrefetchScalarGridSpec(
            num_scalar_prefetch=1,
            grid=(views,),
            in_specs=[
                pl.BlockSpec((1, sources, planes * row_count, columns), lambda v, s: (v, 0, 0, 0)),
                pl.BlockSpec(pool.shape, lambda v, s: (0, 0, 0, 0)),
                pl.BlockSpec((1,) + own.shape[1:], lambda v, s: (v, 0, 0)),
            ],
            out_specs=pl.BlockSpec(
                (1, planes * row_count * groups, columns), lambda v, s: (v, 0, 0)
            ),
            scratch_shapes=[
                pltpu.VMEM((view_count * asked, high * channels, LOW), jnp.bfloat16),
                pltpu.VMEM((sources, planes * row_count, columns), jnp.float32),
                pltpu.VMEM((planes * row_count, columns), jnp.float32),
            ],
        ),
        out_shape=jax.ShapeDtypeStruct(
            (views, planes * row_count * groups, columns), jnp.bfloat16
        ),
        compiler_params=pltpu.CompilerParams(vmem_limit_bytes=40 * 1024 * 1024),
    )(view_lists.reshape(-1), idx, pool, own)

    height = row_count * groups
    slab_planes = planes // depth_count
    padded = jnp.pad(cost, ((0, 0), (height, height), (0, 0)))
    slabs = jnp.stack(
        [
            lax.slice_in_dim(
                padded, t * slab_planes * height, ((t + 1) * slab_planes + 2) * height, axis=1
            )
            for t in range(depth_count)
        ]
    )
    slabs = lax.all_to_all(slabs, "depth", split_axis=0, concat_axis=0, tiled=True)

    place = np.zeros((rows, depth_count, row_count, 3), np.float32)
    for i in range(rows):
        for b in range(3):
            j = i + b - 1
            if 0 <= j < rows:
                place[i, j // row_count, j % row_count, b] = 1.0
    taps = conv_weight.reshape(3, 3, 3, groups, groups)
    band = jnp.einsum(
        "abegh,isrb->ehisarg",
        taps,
        jnp.asarray(place, jnp.bfloat16),
        preferred_element_type=jnp.float32,
    ).astype(jnp.bfloat16)
    band = band.reshape(3 * groups * rows, depth_count * 3 * height)

    return pl.pallas_call(
        functools.partial(conv_kernel, slab_planes, groups, rows),
        grid=(views,),
        in_specs=[
            pl.BlockSpec(
                (depth_count, 1, (slab_planes + 2) * height, columns), lambda v: (0, v, 0, 0)
            ),
            pl.BlockSpec(band.shape, lambda v: (0, 0)),
        ],
        out_specs=pl.BlockSpec(
            (1, groups, slab_planes, rows, columns), lambda v: (v, 0, 0, 0, 0)
        ),
        out_shape=jax.ShapeDtypeStruct(
            (views, groups, slab_planes, rows, columns), jnp.bfloat16
        ),
        compiler_params=pltpu.CompilerParams(vmem_limit_bytes=32 * 1024 * 1024),
    )(slabs, band)


def solution(mesh):
    return jax.shard_map(
        on_device,
        mesh=mesh,
        in_specs=(
            P("view", None, None),
            P("view", None),
            P(),
            P("view", None, None, "depth", None),
            P(),
        ),
        out_specs=P("view", None, "depth", None, None),
        check_vma=False,
    )
```

```python
import functools

import jax
import jax.numpy as jnp
import numpy as np
from jax import lax
from jax.experimental import pallas as pl
from jax.experimental.pallas import tpu as pltpu
from jax.sharding import PartitionSpec as P

LOW = 256


def fetch_kernel(
    asked, ask_ref, tiles_ref, order_ref, pool_ref, stage, send_v, recv_v, send_x, recv_x, send_c, recv_c
):
    views = lax.axis_size("view")
    shares = lax.axis_size("depth")
    lines = shares // 2
    view = lax.axis_index("view")
    depth = lax.axis_index("depth")
    line, core = depth // 2, depth % 2
    other = line * 2 + 1 - core
    width = stage.shape[-1]

    def at_view(step):
        return lax.rem(view + step + views, views)

    def at_line(step):
        return lax.rem(line + step + lines, lines) * 2 + core

    def slots(owner):
        return pl.ds(owner * asked, asked)

    def copy(src, dst, send, recv, where):
        return pltpu.make_async_remote_copy(
            src_ref=src,
            dst_ref=dst,
            send_sem=send,
            recv_sem=recv,
            device_id=where,
            device_id_type=pl.DeviceIdType.MESH,
        )

    barrier = pltpu.get_barrier_semaphore()
    peers = [(at_view(o), depth) for o in range(1, views)]
    peers += [(view, at_line(o)) for o in range(1, lines)]
    peers += [(view, other)]
    for peer in peers:
        pl.semaphore_signal(barrier, inc=1, device_id=peer, device_id_type=pl.DeviceIdType.MESH)

    start = pl.multiple_of(depth * width, width)
    for owner in range(views):
        for c in range(asked):
            tile = tiles_ref[ask_ref[(owner * views + view) * asked + c], :, pl.ds(start, width)]
            moved = jnp.dot(order_ref[...], tile, preferred_element_type=jnp.float32)
            stage[owner, c] = moved.astype(jnp.bfloat16)
    pl.semaphore_wait(barrier, len(peers))

    over_view = []
    for o in range(1, views):
        step = copy(
            stage.at[at_view(o)],
            pool_ref.at[depth, slots(view)],
            send_v.at[o - 1],
            recv_v.at[o - 1],
            (at_view(o), depth),
        )
        step.start()
        over_view.append(step)
    pool_ref[depth, slots(view)] = stage[view]

    over_line, over_core = [], []
    for o in range(views):
        mine = pool_ref.at[depth, slots(at_view(-o))]
        if o > 0:
            copy(
                stage.at[at_view(o)], mine, send_v.at[o - 1], recv_v.at[o - 1], (at_view(o), depth)
            ).wait_recv()
        for x in range(1, lines):
            step = copy(
                mine, mine, send_x.at[x - 1, o], recv_x.at[x - 1, o], (view, at_line(x))
            )
            step.start()
            over_line.append(step)
        step = copy(mine, mine, send_c.at[0, o], recv_c.at[0, o], (view, other))
        step.start()
        over_core.append(step)
    for o in range(views):
        for x in range(1, lines):
            theirs = pool_ref.at[at_line(-x), slots(at_view(-o))]
            copy(
                theirs, theirs, send_x.at[x - 1, o], recv_x.at[x - 1, o], (view, at_line(x))
            ).wait_recv()
            step = copy(theirs, theirs, send_c.at[x, o], recv_c.at[x, o], (view, other))
            step.start()
            over_core.append(step)
    for o in range(views):
        for x in range(lines):
            share = lax.rem(line - x + lines, lines) * 2 + 1 - core
            there = pool_ref.at[share, slots(at_view(-o))]
            copy(there, there, send_c.at[x, o], recv_c.at[x, o], (view, other)).wait_recv()
    for step in over_view + over_line + over_core:
        step.wait_send()


def cost_kernel(
    kinds,
    groups,
    inner,
    source_ref,
    idx_ref,
    pool_ref,
    own_ref,
    slabs_ref,
    cost_ref,
    table_ref,
    low_ref,
    scale_ref,
    send_sem,
    recv_sem,
):
    views, sources, lines, columns = idx_ref.shape
    slots, chans, share = pool_ref.shape[1:]
    high = table_ref.shape[1] // chans
    per = LOW // share
    shares = lax.axis_size("depth")
    view_here = lax.axis_index("view")
    depth = lax.axis_index("depth")
    slab = slabs_ref.shape[2]
    rim = (slab - inner) // 2

    barrier = pltpu.get_barrier_semaphore()
    for o in range(1, shares):
        pl.semaphore_signal(
            barrier,
            inc=1,
            device_id=(view_here, lax.rem(depth + o, shares)),
            device_id_type=pl.DeviceIdType.MESH,
        )

    def one_table(slot, carry):
        parts = [
            jnp.concatenate([pool_ref[h * per + i, slot] for i in range(per)], axis=1)
            for h in range(high)
        ]
        parts = [part.astype(jnp.float32) for part in parts]
        table_ref[slot] = jnp.concatenate(
            [parts[h][t * groups : (t + 1) * groups] for t in range(kinds) for h in range(high)],
            axis=0,
        ).astype(jnp.bfloat16)
        return carry

    lax.fori_loop(0, slots, one_table, 0)
    empty = jnp.zeros((rim, columns), jnp.bfloat16)
    for view in range(views):
        cost_ref[view, :rim] = empty
        cost_ref[view, rim + lines * groups :] = empty

    count = lax.broadcasted_iota(jnp.int32, (LOW, columns), 0).astype(jnp.float32)
    count = count.astype(jnp.bfloat16)
    one = jnp.ones((LOW, columns), jnp.bfloat16)
    zero = jnp.zeros((LOW, columns), jnp.bfloat16)

    def slab_copy(o, view):
        to = lax.rem(depth + o, shares)
        start = pl.multiple_of(to * inner, inner)
        return pltpu.make_async_remote_copy(
            src_ref=cost_ref.at[view, pl.ds(start, slab)],
            dst_ref=slabs_ref.at[depth, view],
            send_sem=send_sem.at[o - 1, view],
            recv_sem=recv_sem.at[o - 1, view],
            device_id=(view_here, to),
            device_id_type=pl.DeviceIdType.MESH,
        )

    def one_view(view, carry):
        live = jnp.zeros(scale_ref.shape, jnp.float32)
        for k in range(sources):
            usable = idx_ref[view, k] >= 0
            low_ref[k] = jnp.where(usable, idx_ref[view, k] & (LOW - 1), -1).astype(jnp.float32)
            live = live + jnp.where(usable, 1.0, 0.0)
        scale_ref[...] = 0.5 / jnp.maximum(live, 1.0)

        def one_pair(pair, carry):
            total = [None] * kinds
            for k in range(sources):
                hots, rows = [], []
                for q in range(2):
                    rows.append(idx_ref[view, k, pl.ds(2 * pair + q, 1), :])
                    low = low_ref[k, pl.ds(2 * pair + q, 1), :]
                    low = jnp.broadcast_to(low, (16, columns)).astype(jnp.bfloat16)
                    low = jnp.concatenate([low] * (LOW // 16), axis=0)
                    hots.append(jnp.where(count == low, one, zero))
                row = jnp.concatenate(rows, axis=1)
                row = jnp.broadcast_to(row, (groups, 2 * columns))
                bits = []
                width = LOW
                while width < LOW * high:
                    bits.append((row & width) != 0)
                    width *= 2
                found = jnp.dot(
                    table_ref[source_ref[view * sources + k]],
                    jnp.concatenate(hots, axis=1),
                    preferred_element_type=jnp.float32,
                )
                for t in range(kinds):
                    first = t * high * groups
                    parts = [
                        found[first + h * groups : first + (h + 1) * groups] for h in range(high)
                    ]
                    for bit in bits:
                        parts = [
                            jnp.where(bit, parts[2 * i + 1], parts[2 * i])
                            for i in range(len(parts) // 2)
                        ]
                    total[t] = parts[0] if k == 0 else total[t] + parts[0]
            summed = None
            for t in range(kinds):
                term = total[t] * own_ref[view, t * groups : (t + 1) * groups, :]
                summed = term if summed is None else summed + term
            cost = [
                summed[:, q * columns : (q + 1) * columns]
                * scale_ref[pl.ds(2 * pair + q, 1), :]
                for q in range(2)
            ]
            start = pl.multiple_of(pair * (2 * groups) + rim, 2 * groups)
            cost_ref[view, pl.ds(start, 2 * groups), :] = jnp.concatenate(cost, axis=0).astype(
                jnp.bfloat16
            )
            return carry

        lax.fori_loop(0, lines // 2, one_pair, 0)

        @pl.when(view == 0)
        def _():
            pl.semaphore_wait(barrier, shares - 1)

        for o in range(1, shares):
            slab_copy(o, view).start()
        start = pl.multiple_of(depth * inner, inner)
        slabs_ref[depth, view] = cost_ref[view, pl.ds(start, slab), :]
        return carry

    lax.fori_loop(0, views, one_view, 0)
    for view in range(views):
        for o in range(1, shares):
            came = lax.rem(depth - o + shares, shares)
            arrived = slabs_ref.at[came, view]
            pltpu.make_async_remote_copy(
                src_ref=arrived,
                dst_ref=arrived,
                send_sem=send_sem.at[o - 1, view],
                recv_sem=recv_sem.at[o - 1, view],
                device_id=(view_here, came),
                device_id_type=pl.DeviceIdType.MESH,
            ).wait_recv()
    for view in range(views):
        for o in range(1, shares):
            slab_copy(o, view).wait_send()


def conv_kernel(planes, groups, rows, edge, slab_ref, taps_ref, out_ref, band_ref):
    shares = slab_ref.shape[0]
    columns = slab_ref.shape[-1]
    height = slab_ref.shape[2] // (planes + 2 * edge)
    out_rows = groups * rows

    @pl.when(pl.program_id(0) == 0)
    def _():
        size = 3 * out_rows
        mix = 3 * groups

        def places(shape, axis):
            return lax.broadcasted_iota(jnp.int32, shape, axis)

        def log(n):
            return n.bit_length() - 1

        spread = (places((size, mix), 0) >> log(rows)) == places((size, mix), 1)
        spread = jnp.where(spread, 1.0, 0.0)
        into, outof = places((mix, size), 0), places((mix, size), 1)
        gather = ((outof >> log(out_rows)) == (into >> log(groups))) & (
            (outof & (groups - 1)) == (into & (groups - 1))
        )
        gather = jnp.where(gather, 1.0, 0.0)
        apart = ((places((size, size), 1) >> log(groups)) & (rows - 1)) - (
            places((size, size), 0) & (rows - 1)
        )
        band = jnp.zeros((size, size), jnp.float32)
        for b in range(3):
            part = jnp.dot(spread, taps_ref[b], preferred_element_type=jnp.float32)
            part = jnp.dot(part, gather, preferred_element_type=jnp.float32)
            band = jnp.where(apart == b - 1, part, band)
        band_ref[...] = band.astype(jnp.bfloat16)

    lane = lax.broadcasted_iota(jnp.int32, (out_rows, columns), 1)
    for first in range(0, planes, 2):
        block = jnp.concatenate(
            [
                jnp.concatenate(
                    [
                        slab_ref[s, 0, (p + a) * height : (p + a + 1) * height, :]
                        for a in range(3)
                        for s in range(shares)
                    ],
                    axis=0,
                )
                for p in (first + edge - 1, first + edge)
            ],
            axis=1,
        )
        mixed = jnp.dot(band_ref[...], block, preferred_element_type=jnp.float32)
        for q in range(2):
            part = mixed[:, q * columns : (q + 1) * columns]
            left = pltpu.roll(part[:out_rows], 1, 1)
            right = pltpu.roll(part[2 * out_rows :], columns - 1, 1)
            total = part[out_rows : 2 * out_rows]
            total = total + jnp.where(lane == 0, 0.0, left)
            total = total + jnp.where(lane == columns - 1, 0.0, right)
            total = total.astype(jnp.bfloat16)
            for h in range(groups):
                out_ref[0, h, first + q] = total[h * rows : (h + 1) * rows]


def on_device(features, view_lists, requests, warp_idx, conv_weight):
    depth_here = lax.axis_index("depth")
    view_count = lax.axis_size("view")
    depth_count = lax.axis_size("depth")
    views, pixels, channels = features.shape
    sources, planes, row_count, columns = warp_idx.shape[1:]
    groups = conv_weight.shape[1]
    kinds = channels // groups
    high = pixels // LOW
    asked = requests.shape[2]
    rows = row_count * depth_count

    lines = depth_count // 2
    share = pixels // depth_count
    order = np.zeros((channels, channels), np.float32)
    for c in range(channels):
        order[(c % kinds) * groups + c // kinds, c] = 1.0
    pool = pl.pallas_call(
        functools.partial(fetch_kernel, asked),
        out_shape=jax.ShapeDtypeStruct(
            (depth_count, view_count * asked, channels, share), jnp.bfloat16
        ),
        in_specs=[
            pl.BlockSpec(memory_space=pltpu.SMEM),
            pl.BlockSpec(memory_space=pltpu.VMEM),
            pl.BlockSpec(memory_space=pltpu.VMEM),
        ],
        out_specs=pl.BlockSpec(memory_space=pltpu.VMEM),
        scratch_shapes=[
            pltpu.VMEM((view_count, asked, channels, share), jnp.bfloat16),
            pltpu.SemaphoreType.DMA((view_count - 1,)),
            pltpu.SemaphoreType.DMA((view_count - 1,)),
            pltpu.SemaphoreType.DMA((lines, view_count)),
            pltpu.SemaphoreType.DMA((lines, view_count)),
            pltpu.SemaphoreType.DMA((lines, view_count)),
            pltpu.SemaphoreType.DMA((lines, view_count)),
        ],
        compiler_params=pltpu.CompilerParams(
            collective_id=0, has_side_effects=True, vmem_limit_bytes=16 * 1024 * 1024
        ),
    )(requests.reshape(-1), features.transpose(0, 2, 1), jnp.asarray(order, jnp.bfloat16))

    own_pixels = row_count * columns
    own = lax.dynamic_slice_in_dim(features, depth_here * own_pixels, own_pixels, 1)
    own = own.reshape(views, own_pixels, groups, kinds).transpose(0, 3, 2, 1)
    own = own.reshape(views, channels, own_pixels).astype(jnp.float32)
    if row_count == 1:
        own = jnp.concatenate([own, own], axis=2)
    idx = warp_idx.reshape(views, sources, planes * row_count, columns)

    height = row_count * groups
    slab_planes = planes // depth_count
    edge = max(1, 16 // height)
    slab = (slab_planes + 2 * edge) * height
    slabs = pl.pallas_call(
        functools.partial(cost_kernel, kinds, groups, slab_planes * height),
        out_shape=jax.ShapeDtypeStruct((depth_count, views, slab, columns), jnp.bfloat16),
        in_specs=[pl.BlockSpec(memory_space=pltpu.SMEM)]
        + [pl.BlockSpec(memory_space=pltpu.VMEM)] * 3,
        out_specs=pl.BlockSpec(memory_space=pltpu.VMEM),
        scratch_shapes=[
            pltpu.VMEM((views, (planes + 2 * edge) * height, columns), jnp.bfloat16),
            pltpu.VMEM((view_count * asked, high * channels, LOW), jnp.bfloat16),
            pltpu.VMEM((sources, planes * row_count, columns), jnp.float32),
            pltpu.VMEM((planes * row_count, columns), jnp.float32),
            pltpu.SemaphoreType.DMA((depth_count - 1, views)),
            pltpu.SemaphoreType.DMA((depth_count - 1, views)),
        ],
        compiler_params=pltpu.CompilerParams(
            collective_id=1, has_side_effects=True, vmem_limit_bytes=40 * 1024 * 1024
        ),
    )(view_lists.reshape(-1), idx, pool, own)

    taps = conv_weight.reshape(3, 3, 3, groups, groups).transpose(1, 2, 4, 0, 3)
    taps = taps.reshape(3, 3 * groups, 3 * groups).astype(jnp.float32)

    return pl.pallas_call(
        functools.partial(conv_kernel, slab_planes, groups, rows, edge),
        grid=(views,),
        in_specs=[
            pl.BlockSpec(
                (depth_count, 1, slab, columns), lambda v: (0, v, 0, 0)
            ),
            pl.BlockSpec(taps.shape, lambda v: (0, 0, 0)),
        ],
        out_specs=pl.BlockSpec(
            (1, groups, slab_planes, rows, columns), lambda v: (v, 0, 0, 0, 0)
        ),
        out_shape=jax.ShapeDtypeStruct(
            (views, groups, slab_planes, rows, columns), jnp.bfloat16
        ),
        scratch_shapes=[pltpu.VMEM((3 * groups * rows, 3 * groups * rows), jnp.bfloat16)],
        compiler_params=pltpu.CompilerParams(vmem_limit_bytes=32 * 1024 * 1024),
    )(slabs, taps)


def solution(mesh):
    return jax.shard_map(
        on_device,
        mesh=mesh,
        in_specs=(
            P("view", None, None),
            P("view", None),
            P(),
            P("view", None, None, "depth", None),
            P(),
        ),
        out_specs=P("view", None, "depth", None, None),
        check_vma=False,
    )
```

```python
import functools

import jax
import jax.numpy as jnp
import numpy as np
from jax import lax
from jax.experimental import pallas as pl
from jax.experimental.pallas import tpu as pltpu
from jax.sharding import PartitionSpec as P

LOW = 256


def fetch_kernel(
    asked, ask_ref, tiles_ref, order_ref, pool_ref, own_ref, stage, send_v, recv_v, send_x, recv_x, send_c, recv_c
):
    views = lax.axis_size("view")
    shares = lax.axis_size("depth")
    lines = shares // 2
    view = lax.axis_index("view")
    depth = lax.axis_index("depth")
    line, core = depth // 2, depth % 2
    other = line * 2 + 1 - core
    width = stage.shape[-1]

    def at_view(step):
        return lax.rem(view + step + views, views)

    def at_line(step):
        return lax.rem(line + step + lines, lines) * 2 + core

    def slots(owner):
        return pl.ds(owner * asked, asked)

    def copy(src, dst, send, recv, where):
        return pltpu.make_async_remote_copy(
            src_ref=src,
            dst_ref=dst,
            send_sem=send,
            recv_sem=recv,
            device_id=where,
            device_id_type=pl.DeviceIdType.MESH,
        )

    barrier = pltpu.get_barrier_semaphore()
    peers = [(at_view(o), depth) for o in range(1, views)]
    peers += [(view, at_line(o)) for o in range(1, lines)]
    peers += [(view, other)]
    for peer in peers:
        pl.semaphore_signal(barrier, inc=1, device_id=peer, device_id_type=pl.DeviceIdType.MESH)

    start = pl.multiple_of(depth * width, width)
    for owner in range(views):
        for c in range(asked):
            tile = tiles_ref[ask_ref[(owner * views + view) * asked + c], :, pl.ds(start, width)]
            moved = jnp.dot(order_ref[...], tile, preferred_element_type=jnp.float32)
            stage[owner, c] = moved.astype(jnp.bfloat16)
    for tile in range(tiles_ref.shape[0]):
        part = tiles_ref[tile, :, pl.ds(start, width)]
        part = jnp.dot(order_ref[...], part, preferred_element_type=jnp.float32)
        for i in range(own_ref.shape[-1] // width):
            own_ref[tile, :, i * width : (i + 1) * width] = part
    pl.semaphore_wait(barrier, len(peers))

    over_view = []
    for o in range(1, views):
        step = copy(
            stage.at[at_view(o)],
            pool_ref.at[depth, slots(view)],
            send_v.at[o - 1],
            recv_v.at[o - 1],
            (at_view(o), depth),
        )
        step.start()
        over_view.append(step)
    pool_ref[depth, slots(view)] = stage[view]

    over_line, over_core = [], []
    for o in range(views):
        mine = pool_ref.at[depth, slots(at_view(-o))]
        if o > 0:
            copy(
                stage.at[at_view(o)], mine, send_v.at[o - 1], recv_v.at[o - 1], (at_view(o), depth)
            ).wait_recv()
        for x in range(1, lines):
            step = copy(
                mine, mine, send_x.at[x - 1, o], recv_x.at[x - 1, o], (view, at_line(x))
            )
            step.start()
            over_line.append(step)
        step = copy(mine, mine, send_c.at[0, o], recv_c.at[0, o], (view, other))
        step.start()
        over_core.append(step)
    for o in range(views):
        for x in range(1, lines):
            theirs = pool_ref.at[at_line(-x), slots(at_view(-o))]
            copy(
                theirs, theirs, send_x.at[x - 1, o], recv_x.at[x - 1, o], (view, at_line(x))
            ).wait_recv()
            step = copy(theirs, theirs, send_c.at[x, o], recv_c.at[x, o], (view, other))
            step.start()
            over_core.append(step)
    for o in range(views):
        for x in range(lines):
            share = lax.rem(line - x + lines, lines) * 2 + 1 - core
            there = pool_ref.at[share, slots(at_view(-o))]
            copy(there, there, send_c.at[x, o], recv_c.at[x, o], (view, other)).wait_recv()
    for step in over_view + over_line + over_core:
        step.wait_send()


def cost_kernel(
    kinds,
    groups,
    inner,
    source_ref,
    idx_ref,
    pool_ref,
    own_ref,
    slabs_ref,
    cost_ref,
    table_ref,
    low_ref,
    scale_ref,
    send_sem,
    recv_sem,
):
    views, sources, lines, columns = idx_ref.shape
    slots, chans, share = pool_ref.shape[1:]
    high = table_ref.shape[1] // chans
    per = LOW // share
    shares = lax.axis_size("depth")
    view_here = lax.axis_index("view")
    depth = lax.axis_index("depth")
    slab = slabs_ref.shape[2]
    rim = (slab - inner) // 2

    barrier = pltpu.get_barrier_semaphore()
    for o in range(1, shares):
        pl.semaphore_signal(
            barrier,
            inc=1,
            device_id=(view_here, lax.rem(depth + o, shares)),
            device_id_type=pl.DeviceIdType.MESH,
        )

    def one_table(slot, carry):
        parts = [
            jnp.concatenate([pool_ref[h * per + i, slot] for i in range(per)], axis=1)
            for h in range(high)
        ]
        parts = [part.astype(jnp.float32) for part in parts]
        table_ref[slot] = jnp.concatenate(
            [parts[h][t * groups : (t + 1) * groups] for t in range(kinds) for h in range(high)],
            axis=0,
        ).astype(jnp.bfloat16)
        return carry

    lax.fori_loop(0, slots, one_table, 0)
    empty = jnp.zeros((rim, columns), jnp.bfloat16)
    for view in range(views):
        cost_ref[view, :rim] = empty
        cost_ref[view, rim + lines * groups :] = empty

    count = lax.broadcasted_iota(jnp.int32, (LOW, columns), 0).astype(jnp.float32)
    count = count.astype(jnp.bfloat16)
    one = jnp.ones((LOW, columns), jnp.bfloat16)
    zero = jnp.zeros((LOW, columns), jnp.bfloat16)

    def slab_copy(o, view):
        to = lax.rem(depth + o, shares)
        start = pl.multiple_of(to * inner, inner)
        return pltpu.make_async_remote_copy(
            src_ref=cost_ref.at[view, pl.ds(start, slab)],
            dst_ref=slabs_ref.at[depth, view],
            send_sem=send_sem.at[o - 1, view],
            recv_sem=recv_sem.at[o - 1, view],
            device_id=(view_here, to),
            device_id_type=pl.DeviceIdType.MESH,
        )

    def one_view(view, carry):
        live = jnp.zeros(scale_ref.shape, jnp.float32)
        for k in range(sources):
            usable = idx_ref[view, k] >= 0
            low_ref[k] = jnp.where(usable, idx_ref[view, k] & (LOW - 1), -1).astype(jnp.float32)
            live = live + jnp.where(usable, 1.0, 0.0)
        scale_ref[...] = 0.5 / jnp.maximum(live, 1.0)

        def one_pair(pair, carry):
            total = [None] * kinds
            for k in range(sources):
                hots, rows = [], []
                for q in range(2):
                    rows.append(idx_ref[view, k, pl.ds(2 * pair + q, 1), :])
                    low = low_ref[k, pl.ds(2 * pair + q, 1), :]
                    low = jnp.broadcast_to(low, (16, columns)).astype(jnp.bfloat16)
                    low = jnp.concatenate([low] * (LOW // 16), axis=0)
                    hots.append(jnp.where(count == low, one, zero))
                row = jnp.concatenate(rows, axis=1)
                row = jnp.broadcast_to(row, (groups, 2 * columns))
                bits = []
                width = LOW
                while width < LOW * high:
                    bits.append((row & width) != 0)
                    width *= 2
                found = jnp.dot(
                    table_ref[source_ref[view * sources + k]],
                    jnp.concatenate(hots, axis=1),
                    preferred_element_type=jnp.float32,
                )
                for t in range(kinds):
                    first = t * high * groups
                    parts = [
                        found[first + h * groups : first + (h + 1) * groups] for h in range(high)
                    ]
                    for bit in bits:
                        parts = [
                            jnp.where(bit, parts[2 * i + 1], parts[2 * i])
                            for i in range(len(parts) // 2)
                        ]
                    total[t] = parts[0] if k == 0 else total[t] + parts[0]
            summed = None
            for t in range(kinds):
                term = total[t] * own_ref[view, t * groups : (t + 1) * groups, :]
                summed = term if summed is None else summed + term
            cost = [
                summed[:, q * columns : (q + 1) * columns]
                * scale_ref[pl.ds(2 * pair + q, 1), :]
                for q in range(2)
            ]
            start = pl.multiple_of(pair * (2 * groups) + rim, 2 * groups)
            cost_ref[view, pl.ds(start, 2 * groups), :] = jnp.concatenate(cost, axis=0).astype(
                jnp.bfloat16
            )
            return carry

        lax.fori_loop(0, lines // 2, one_pair, 0, unroll=4)

        @pl.when(view == 0)
        def _():
            pl.semaphore_wait(barrier, shares - 1)

        for o in range(1, shares):
            slab_copy(o, view).start()
        start = pl.multiple_of(depth * inner, inner)
        slabs_ref[depth, view] = cost_ref[view, pl.ds(start, slab), :]
        return carry

    lax.fori_loop(0, views, one_view, 0)
    for view in range(views):
        for o in range(1, shares):
            came = lax.rem(depth - o + shares, shares)
            arrived = slabs_ref.at[came, view]
            pltpu.make_async_remote_copy(
                src_ref=arrived,
                dst_ref=arrived,
                send_sem=send_sem.at[o - 1, view],
                recv_sem=recv_sem.at[o - 1, view],
                device_id=(view_here, came),
                device_id_type=pl.DeviceIdType.MESH,
            ).wait_recv()
    for view in range(views):
        for o in range(1, shares):
            slab_copy(o, view).wait_send()


def conv_kernel(planes, groups, rows, edge, slab_ref, taps_ref, out_ref, band_ref):
    shares = slab_ref.shape[0]
    columns = slab_ref.shape[-1]
    height = slab_ref.shape[2] // (planes + 2 * edge)
    out_rows = groups * rows

    @pl.when(pl.program_id(0) == 0)
    def _():
        size = 3 * out_rows
        mix = 3 * groups

        def places(shape, axis):
            return lax.broadcasted_iota(jnp.int32, shape, axis)

        def log(n):
            return n.bit_length() - 1

        spread = (places((size, mix), 0) >> log(rows)) == places((size, mix), 1)
        spread = jnp.where(spread, 1.0, 0.0)
        into, outof = places((mix, size), 0), places((mix, size), 1)
        gather = ((outof >> log(out_rows)) == (into >> log(groups))) & (
            (outof & (groups - 1)) == (into & (groups - 1))
        )
        gather = jnp.where(gather, 1.0, 0.0)
        apart = ((places((size, size), 1) >> log(groups)) & (rows - 1)) - (
            places((size, size), 0) & (rows - 1)
        )
        band = jnp.zeros((size, size), jnp.float32)
        for b in range(3):
            part = jnp.dot(spread, taps_ref[b], preferred_element_type=jnp.float32)
            part = jnp.dot(part, gather, preferred_element_type=jnp.float32)
            band = jnp.where(apart == b - 1, part, band)
        band_ref[...] = band.astype(jnp.bfloat16)

    lane = lax.broadcasted_iota(jnp.int32, (out_rows, columns), 1)
    for first in range(0, planes, 2):
        block = jnp.concatenate(
            [
                jnp.concatenate(
                    [
                        slab_ref[s, 0, (p + a) * height : (p + a + 1) * height, :]
                        for a in range(3)
                        for s in range(shares)
                    ],
                    axis=0,
                )
                for p in (first + edge - 1, first + edge)
            ],
            axis=1,
        )
        mixed = jnp.dot(band_ref[...], block, preferred_element_type=jnp.float32)
        for q in range(2):
            part = mixed[:, q * columns : (q + 1) * columns]
            left = pltpu.roll(part[:out_rows], 1, 1)
            right = pltpu.roll(part[2 * out_rows :], columns - 1, 1)
            total = part[out_rows : 2 * out_rows]
            total = total + jnp.where(lane == 0, 0.0, left)
            total = total + jnp.where(lane == columns - 1, 0.0, right)
            total = total.astype(jnp.bfloat16)
            for h in range(groups):
                out_ref[0, h, first + q] = total[h * rows : (h + 1) * rows]


def on_device(features, view_lists, requests, warp_idx, conv_weight):
    view_count = lax.axis_size("view")
    depth_count = lax.axis_size("depth")
    views, pixels, channels = features.shape
    sources, planes, row_count, columns = warp_idx.shape[1:]
    groups = conv_weight.shape[1]
    kinds = channels // groups
    high = pixels // LOW
    asked = requests.shape[2]
    rows = row_count * depth_count

    lines = depth_count // 2
    share = pixels // depth_count
    order = np.zeros((channels, channels), np.float32)
    for c in range(channels):
        order[(c % kinds) * groups + c // kinds, c] = 1.0
    pool, own = pl.pallas_call(
        functools.partial(fetch_kernel, asked),
        out_shape=(
            jax.ShapeDtypeStruct(
                (depth_count, view_count * asked, channels, share), jnp.bfloat16
            ),
            jax.ShapeDtypeStruct((views, channels, 2 * columns), jnp.float32),
        ),
        in_specs=[
            pl.BlockSpec(memory_space=pltpu.SMEM),
            pl.BlockSpec(memory_space=pltpu.VMEM),
            pl.BlockSpec(memory_space=pltpu.VMEM),
        ],
        out_specs=(pl.BlockSpec(memory_space=pltpu.VMEM),) * 2,
        scratch_shapes=[
            pltpu.VMEM((view_count, asked, channels, share), jnp.bfloat16),
            pltpu.SemaphoreType.DMA((view_count - 1,)),
            pltpu.SemaphoreType.DMA((view_count - 1,)),
            pltpu.SemaphoreType.DMA((lines, view_count)),
            pltpu.SemaphoreType.DMA((lines, view_count)),
            pltpu.SemaphoreType.DMA((lines, view_count)),
            pltpu.SemaphoreType.DMA((lines, view_count)),
        ],
        compiler_params=pltpu.CompilerParams(
            collective_id=0, has_side_effects=True, vmem_limit_bytes=16 * 1024 * 1024
        ),
    )(requests.reshape(-1), features.transpose(0, 2, 1), jnp.asarray(order, jnp.bfloat16))

    idx = warp_idx.reshape(views, sources, planes * row_count, columns)

    height = row_count * groups
    slab_planes = planes // depth_count
    edge = max(1, 16 // height)
    slab = (slab_planes + 2 * edge) * height
    slabs = pl.pallas_call(
        functools.partial(cost_kernel, kinds, groups, slab_planes * height),
        out_shape=jax.ShapeDtypeStruct((depth_count, views, slab, columns), jnp.bfloat16),
        in_specs=[pl.BlockSpec(memory_space=pltpu.SMEM)]
        + [pl.BlockSpec(memory_space=pltpu.VMEM)] * 3,
        out_specs=pl.BlockSpec(memory_space=pltpu.VMEM),
        scratch_shapes=[
            pltpu.VMEM((views, (planes + 2 * edge) * height, columns), jnp.bfloat16),
            pltpu.VMEM((view_count * asked, high * channels, LOW), jnp.bfloat16),
            pltpu.VMEM((sources, planes * row_count, columns), jnp.float32),
            pltpu.VMEM((planes * row_count, columns), jnp.float32),
            pltpu.SemaphoreType.DMA((depth_count - 1, views)),
            pltpu.SemaphoreType.DMA((depth_count - 1, views)),
        ],
        compiler_params=pltpu.CompilerParams(
            collective_id=1, has_side_effects=True, vmem_limit_bytes=40 * 1024 * 1024
        ),
    )(view_lists.reshape(-1), idx, pool, own)

    taps = conv_weight.reshape(3, 3, 3, groups, groups).transpose(1, 2, 4, 0, 3)
    taps = taps.reshape(3, 3 * groups, 3 * groups).astype(jnp.float32)

    return pl.pallas_call(
        functools.partial(conv_kernel, slab_planes, groups, rows, edge),
        grid=(views,),
        in_specs=[
            pl.BlockSpec(
                (depth_count, 1, slab, columns), lambda v: (0, v, 0, 0)
            ),
            pl.BlockSpec(taps.shape, lambda v: (0, 0, 0)),
        ],
        out_specs=pl.BlockSpec(
            (1, groups, slab_planes, rows, columns), lambda v: (v, 0, 0, 0, 0)
        ),
        out_shape=jax.ShapeDtypeStruct(
            (views, groups, slab_planes, rows, columns), jnp.bfloat16
        ),
        scratch_shapes=[pltpu.VMEM((3 * groups * rows, 3 * groups * rows), jnp.bfloat16)],
        compiler_params=pltpu.CompilerParams(vmem_limit_bytes=32 * 1024 * 1024),
    )(slabs, taps)


def solution(mesh):
    return jax.shard_map(
        on_device,
        mesh=mesh,
        in_specs=(
            P("view", None, None),
            P("view", None),
            P(),
            P("view", None, None, "depth", None),
            P(),
        ),
        out_specs=P("view", None, "depth", None, None),
        check_vma=False,
    )
```

```python
import functools

import jax
import jax.numpy as jnp
import numpy as np
from jax import lax
from jax.experimental import pallas as pl
from jax.experimental.pallas import tpu as pltpu
from jax.sharding import PartitionSpec as P

LOW = 256


def fetch_kernel(
    asked, ask_ref, tiles_ref, order_ref, pool_ref, own_ref, stage, send_v, recv_v, send_x, recv_x, send_c, recv_c
):
    views = lax.axis_size("view")
    shares = lax.axis_size("depth")
    lines = shares // 2
    view = lax.axis_index("view")
    depth = lax.axis_index("depth")
    line, core = depth // 2, depth % 2
    other = line * 2 + 1 - core
    width = stage.shape[-1]

    def at_view(step):
        return lax.rem(view + step + views, views)

    def at_line(step):
        return lax.rem(line + step + lines, lines) * 2 + core

    def slots(owner):
        return pl.ds(owner * asked, asked)

    def copy(src, dst, send, recv, where):
        return pltpu.make_async_remote_copy(
            src_ref=src,
            dst_ref=dst,
            send_sem=send,
            recv_sem=recv,
            device_id=where,
            device_id_type=pl.DeviceIdType.MESH,
        )

    barrier = pltpu.get_barrier_semaphore()
    peers = [(at_view(o), depth) for o in range(1, views)]
    peers += [(view, lax.rem(depth + o, shares)) for o in range(1, shares)]
    for peer in peers:
        pl.semaphore_signal(barrier, inc=1, device_id=peer, device_id_type=pl.DeviceIdType.MESH)

    start = pl.multiple_of(depth * width, width)
    for owner in range(views):
        for c in range(asked):
            tile = tiles_ref[ask_ref[(owner * views + view) * asked + c], :, pl.ds(start, width)]
            moved = jnp.dot(order_ref[...], tile, preferred_element_type=jnp.float32)
            stage[owner, c] = moved.astype(jnp.bfloat16)
    for tile in range(tiles_ref.shape[0]):
        part = tiles_ref[tile, :, pl.ds(start, width)]
        part = jnp.dot(order_ref[...], part, preferred_element_type=jnp.float32)
        for i in range(own_ref.shape[-1] // width):
            own_ref[tile, :, i * width : (i + 1) * width] = part
    pl.semaphore_wait(barrier, len(peers))

    over_view = []
    for o in range(1, views):
        step = copy(
            stage.at[at_view(o)],
            pool_ref.at[depth, slots(view)],
            send_v.at[o - 1],
            recv_v.at[o - 1],
            (at_view(o), depth),
        )
        step.start()
        over_view.append(step)
    pool_ref[depth, slots(view)] = stage[view]

    over_line, over_core = [], []
    for o in range(views):
        mine = pool_ref.at[depth, slots(at_view(-o))]
        if o > 0:
            copy(
                stage.at[at_view(o)], mine, send_v.at[o - 1], recv_v.at[o - 1], (at_view(o), depth)
            ).wait_recv()
        for x in range(1, lines):
            step = copy(
                mine, mine, send_x.at[x - 1, o], recv_x.at[x - 1, o], (view, at_line(x))
            )
            step.start()
            over_line.append(step)
        step = copy(mine, mine, send_c.at[0, o], recv_c.at[0, o], (view, other))
        step.start()
        over_core.append(step)
    for o in range(views):
        for x in range(1, lines):
            theirs = pool_ref.at[at_line(-x), slots(at_view(-o))]
            copy(
                theirs, theirs, send_x.at[x - 1, o], recv_x.at[x - 1, o], (view, at_line(x))
            ).wait_recv()
            step = copy(theirs, theirs, send_c.at[x, o], recv_c.at[x, o], (view, other))
            step.start()
            over_core.append(step)
    for o in range(views):
        for x in range(lines):
            share = lax.rem(line - x + lines, lines) * 2 + 1 - core
            there = pool_ref.at[share, slots(at_view(-o))]
            copy(there, there, send_c.at[x, o], recv_c.at[x, o], (view, other)).wait_recv()
    for step in over_view + over_line + over_core:
        step.wait_send()


def cost_kernel(
    kinds,
    groups,
    inner,
    source_ref,
    idx_ref,
    pool_ref,
    own_ref,
    slabs_ref,
    cost_ref,
    table_ref,
    low_ref,
    scale_ref,
    send_sem,
    recv_sem,
):
    views, sources, lines, columns = idx_ref.shape
    slots, chans, share = pool_ref.shape[1:]
    high = table_ref.shape[1] // chans
    per = LOW // share
    shares = lax.axis_size("depth")
    view_here = lax.axis_index("view")
    depth = lax.axis_index("depth")
    slab = slabs_ref.shape[2]
    rim = (slab - inner) // 2

    def one_table(slot, carry):
        parts = [
            jnp.concatenate([pool_ref[h * per + i, slot] for i in range(per)], axis=1)
            for h in range(high)
        ]
        parts = [part.astype(jnp.float32) for part in parts]
        table_ref[slot] = jnp.concatenate(
            [parts[h][t * groups : (t + 1) * groups] for t in range(kinds) for h in range(high)],
            axis=0,
        ).astype(jnp.bfloat16)
        return carry

    lax.fori_loop(0, slots, one_table, 0)
    empty = jnp.zeros((rim, columns), jnp.bfloat16)
    for view in range(views):
        cost_ref[view, :rim] = empty
        cost_ref[view, rim + lines * groups :] = empty

    count = lax.broadcasted_iota(jnp.int32, (LOW, columns), 0).astype(jnp.float32)
    count = count.astype(jnp.bfloat16)
    one = jnp.ones((LOW, columns), jnp.bfloat16)
    zero = jnp.zeros((LOW, columns), jnp.bfloat16)

    def slab_copy(o, view):
        to = lax.rem(depth + o, shares)
        start = pl.multiple_of(to * inner, inner)
        return pltpu.make_async_remote_copy(
            src_ref=cost_ref.at[view, pl.ds(start, slab)],
            dst_ref=slabs_ref.at[depth, view],
            send_sem=send_sem.at[o - 1, view],
            recv_sem=recv_sem.at[o - 1, view],
            device_id=(view_here, to),
            device_id_type=pl.DeviceIdType.MESH,
        )

    def one_view(view, carry):
        live = jnp.zeros(scale_ref.shape, jnp.float32)
        for k in range(sources):
            usable = idx_ref[view, k] >= 0
            low_ref[k] = jnp.where(usable, idx_ref[view, k] & (LOW - 1), -1).astype(jnp.float32)
            live = live + jnp.where(usable, 1.0, 0.0)
        scale_ref[...] = 0.5 / jnp.maximum(live, 1.0)

        def one_pair(pair, carry):
            total = [None] * kinds
            for k in range(sources):
                hots, rows = [], []
                for q in range(2):
                    rows.append(idx_ref[view, k, pl.ds(2 * pair + q, 1), :])
                    low = low_ref[k, pl.ds(2 * pair + q, 1), :]
                    low = jnp.broadcast_to(low, (16, columns)).astype(jnp.bfloat16)
                    low = jnp.concatenate([low] * (LOW // 16), axis=0)
                    hots.append(jnp.where(count == low, one, zero))
                row = jnp.concatenate(rows, axis=1)
                row = jnp.broadcast_to(row, (groups, 2 * columns))
                bits = []
                width = LOW
                while width < LOW * high:
                    bits.append((row & width) != 0)
                    width *= 2
                found = jnp.dot(
                    table_ref[source_ref[view * sources + k]],
                    jnp.concatenate(hots, axis=1),
                    preferred_element_type=jnp.float32,
                )
                for t in range(kinds):
                    first = t * high * groups
                    parts = [
                        found[first + h * groups : first + (h + 1) * groups] for h in range(high)
                    ]
                    for bit in bits:
                        parts = [
                            jnp.where(bit, parts[2 * i + 1], parts[2 * i])
                            for i in range(len(parts) // 2)
                        ]
                    total[t] = parts[0] if k == 0 else total[t] + parts[0]
            summed = None
            for t in range(kinds):
                term = total[t] * own_ref[view, t * groups : (t + 1) * groups, :]
                summed = term if summed is None else summed + term
            cost = [
                summed[:, q * columns : (q + 1) * columns]
                * scale_ref[pl.ds(2 * pair + q, 1), :]
                for q in range(2)
            ]
            start = pl.multiple_of(pair * (2 * groups) + rim, 2 * groups)
            cost_ref[view, pl.ds(start, 2 * groups), :] = jnp.concatenate(cost, axis=0).astype(
                jnp.bfloat16
            )
            return carry

        lax.fori_loop(0, lines // 2, one_pair, 0, unroll=min(16, lines // 2))

        for o in range(1, shares):
            slab_copy(o, view).start()
        start = pl.multiple_of(depth * inner, inner)
        slabs_ref[depth, view] = cost_ref[view, pl.ds(start, slab), :]
        return carry

    lax.fori_loop(0, views, one_view, 0)
    for view in range(views):
        for o in range(1, shares):
            came = lax.rem(depth - o + shares, shares)
            arrived = slabs_ref.at[came, view]
            pltpu.make_async_remote_copy(
                src_ref=arrived,
                dst_ref=arrived,
                send_sem=send_sem.at[o - 1, view],
                recv_sem=recv_sem.at[o - 1, view],
                device_id=(view_here, came),
                device_id_type=pl.DeviceIdType.MESH,
            ).wait_recv()
    for view in range(views):
        for o in range(1, shares):
            slab_copy(o, view).wait_send()


def fetch_and_cost(
    asked,
    kinds,
    groups,
    inner,
    ask_ref,
    source_ref,
    tiles_ref,
    order_ref,
    far_idx_ref,
    slabs_ref,
    idx_ref,
    idx_sem,
    pool_ref,
    own_ref,
    *scratch,
):
    indices = pltpu.make_async_copy(far_idx_ref, idx_ref, idx_sem)
    indices.start()
    fetch_kernel(asked, ask_ref, tiles_ref, order_ref, pool_ref, own_ref, *scratch[:7])
    indices.wait()
    cost_kernel(
        kinds, groups, inner, source_ref, idx_ref, pool_ref, own_ref, slabs_ref, *scratch[7:]
    )


def conv_kernel(planes, groups, rows, edge, slab_ref, taps_ref, out_ref, band_ref):
    shares = slab_ref.shape[0]
    columns = slab_ref.shape[-1]
    height = slab_ref.shape[2] // (planes + 2 * edge)
    out_rows = groups * rows

    @pl.when(pl.program_id(0) == 0)
    def _():
        size = 3 * out_rows
        mix = 3 * groups

        def places(shape, axis):
            return lax.broadcasted_iota(jnp.int32, shape, axis)

        def log(n):
            return n.bit_length() - 1

        spread = (places((size, mix), 0) >> log(rows)) == places((size, mix), 1)
        spread = jnp.where(spread, 1.0, 0.0)
        into, outof = places((mix, size), 0), places((mix, size), 1)
        gather = ((outof >> log(out_rows)) == (into >> log(groups))) & (
            (outof & (groups - 1)) == (into & (groups - 1))
        )
        gather = jnp.where(gather, 1.0, 0.0)
        apart = ((places((size, size), 1) >> log(groups)) & (rows - 1)) - (
            places((size, size), 0) & (rows - 1)
        )
        band = jnp.zeros((size, size), jnp.float32)
        for b in range(3):
            part = jnp.dot(spread, taps_ref[b], preferred_element_type=jnp.float32)
            part = jnp.dot(part, gather, preferred_element_type=jnp.float32)
            band = jnp.where(apart == b - 1, part, band)
        band_ref[...] = band.astype(jnp.bfloat16)

    lane = lax.broadcasted_iota(jnp.int32, (out_rows, columns), 1)
    for first in range(0, planes, 2):
        block = jnp.concatenate(
            [
                jnp.concatenate(
                    [
                        slab_ref[s, 0, (p + a) * height : (p + a + 1) * height, :]
                        for a in range(3)
                        for s in range(shares)
                    ],
                    axis=0,
                )
                for p in (first + edge - 1, first + edge)
            ],
            axis=1,
        )
        mixed = jnp.dot(band_ref[...], block, preferred_element_type=jnp.float32)
        for q in range(2):
            part = mixed[:, q * columns : (q + 1) * columns]
            left = pltpu.roll(part[:out_rows], 1, 1)
            right = pltpu.roll(part[2 * out_rows :], columns - 1, 1)
            total = part[out_rows : 2 * out_rows]
            total = total + jnp.where(lane == 0, 0.0, left)
            total = total + jnp.where(lane == columns - 1, 0.0, right)
            total = total.astype(jnp.bfloat16)
            for h in range(groups):
                out_ref[0, h, first + q] = total[h * rows : (h + 1) * rows]


def on_device(features, view_lists, requests, warp_idx, conv_weight):
    view_count = lax.axis_size("view")
    depth_count = lax.axis_size("depth")
    views, pixels, channels = features.shape
    sources, planes, row_count, columns = warp_idx.shape[1:]
    groups = conv_weight.shape[1]
    kinds = channels // groups
    high = pixels // LOW
    asked = requests.shape[2]
    rows = row_count * depth_count

    lines = depth_count // 2
    share = pixels // depth_count
    order = np.zeros((channels, channels), np.float32)
    for c in range(channels):
        order[(c % kinds) * groups + c // kinds, c] = 1.0
    idx = warp_idx.reshape(views, sources, planes * row_count, columns)
    height = row_count * groups
    slab_planes = planes // depth_count
    edge = max(1, 16 // height)
    slab = (slab_planes + 2 * edge) * height
    slabs = pl.pallas_call(
        functools.partial(fetch_and_cost, asked, kinds, groups, slab_planes * height),
        out_shape=jax.ShapeDtypeStruct((depth_count, views, slab, columns), jnp.bfloat16),
        in_specs=[
            pl.BlockSpec(memory_space=pltpu.SMEM),
            pl.BlockSpec(memory_space=pltpu.SMEM),
            pl.BlockSpec(memory_space=pltpu.VMEM),
            pl.BlockSpec(memory_space=pltpu.VMEM),
            pl.BlockSpec(memory_space=pl.ANY),
        ],
        out_specs=pl.BlockSpec(memory_space=pltpu.VMEM),
        scratch_shapes=[
            pltpu.VMEM(idx.shape, jnp.int32),
            pltpu.SemaphoreType.DMA,
            pltpu.VMEM((depth_count, view_count * asked, channels, share), jnp.bfloat16),
            pltpu.VMEM((views, channels, 2 * columns), jnp.float32),
            pltpu.VMEM((view_count, asked, channels, share), jnp.bfloat16),
            pltpu.SemaphoreType.DMA((view_count - 1,)),
            pltpu.SemaphoreType.DMA((view_count - 1,)),
            pltpu.SemaphoreType.DMA((lines, view_count)),
            pltpu.SemaphoreType.DMA((lines, view_count)),
            pltpu.SemaphoreType.DMA((lines, view_count)),
            pltpu.SemaphoreType.DMA((lines, view_count)),
            pltpu.VMEM((views, (planes + 2 * edge) * height, columns), jnp.bfloat16),
            pltpu.VMEM((view_count * asked, high * channels, LOW), jnp.bfloat16),
            pltpu.VMEM((sources, planes * row_count, columns), jnp.float32),
            pltpu.VMEM((planes * row_count, columns), jnp.float32),
            pltpu.SemaphoreType.DMA((depth_count - 1, views)),
            pltpu.SemaphoreType.DMA((depth_count - 1, views)),
        ],
        compiler_params=pltpu.CompilerParams(
            collective_id=0, has_side_effects=True, vmem_limit_bytes=48 * 1024 * 1024
        ),
    )(
        requests.reshape(-1),
        view_lists.reshape(-1),
        features.transpose(0, 2, 1),
        jnp.asarray(order, jnp.bfloat16),
        idx,
    )

    taps = conv_weight.reshape(3, 3, 3, groups, groups).transpose(1, 2, 4, 0, 3)
    taps = taps.reshape(3, 3 * groups, 3 * groups).astype(jnp.float32)

    return pl.pallas_call(
        functools.partial(conv_kernel, slab_planes, groups, rows, edge),
        grid=(views,),
        in_specs=[
            pl.BlockSpec(
                (depth_count, 1, slab, columns), lambda v: (0, v, 0, 0)
            ),
            pl.BlockSpec(taps.shape, lambda v: (0, 0, 0)),
        ],
        out_specs=pl.BlockSpec(
            (1, groups, slab_planes, rows, columns), lambda v: (v, 0, 0, 0, 0)
        ),
        out_shape=jax.ShapeDtypeStruct(
            (views, groups, slab_planes, rows, columns), jnp.bfloat16
        ),
        scratch_shapes=[pltpu.VMEM((3 * groups * rows, 3 * groups * rows), jnp.bfloat16)],
        compiler_params=pltpu.CompilerParams(vmem_limit_bytes=32 * 1024 * 1024),
    )(slabs, taps)


def solution(mesh):
    return jax.shard_map(
        on_device,
        mesh=mesh,
        in_specs=(
            P("view", None, None),
            P("view", None),
            P(),
            P("view", None, None, "depth", None),
            P(),
        ),
        out_specs=P("view", None, "depth", None, None),
        check_vma=False,
    )
```
